32 devices in a mesh: space: 4 (over y, core), snap: 8 (over z, x).
Axes of the slice: x: 2, y: 2, z: 4, core: 2. Of those that a mesh axis runs over, the one named last changes fastest.
Arguments:
- snapshots: bfloat16 [8192, 4096], P('space', 'snap'), may hold values from -6 to 6
- volume: float32 [8192], P('space'), may hold values from 0.25 to 4
- masks: int32 [4], replicated, may hold values from 1 to 7, as said below
Outputs:
- cross_gram: float32 [4, 8, 512, 512], P(None, 'snap', 'space')
The draws below stay inside these ranges and needn't reach their ends.
Inputs may be any that keep to these rules, and one draw needn't show every extreme that they name: `masks`: all values are distinct; the first has exactly one bit set, and each later value differs from the one before in exactly one bit.
All inputs are finite; a program needn't handle non-finite values.
Results may differ from the reference program's by a relative error of at most 0.0041.
Values may be sent and summed in bfloat16 or wider, within the bound.
No kernel may reach another device: no remote copies, remote signals or barrier semaphores. Data moves between devices by JAX's collectives and lax.ppermute only.
A program may use at most 64 MiB of HBM per device.

```python
import math
import jax
import jax.numpy as jnp
from jax import lax

GROUP = 512
ROUNDS = 4
GROUPS = 8
SNAPS = 4096
CELLS = 8192


def draw_masks(key, part):
    key = jax.random.fold_in(key, 7)
    bit_count = GROUPS.bit_length() - 1
    bit_order = jax.random.permutation(key, bit_count).astype(jnp.int32)
    collected = []
    total_mask = jnp.int32(0)
    for round_number in range(ROUNDS):
        if round_number < bit_count:
            position = round_number
        else:
            position = round_number - bit_count
        total_mask = jnp.bitwise_xor(total_mask, jnp.left_shift(jnp.int32(1), bit_order[position]))
        collected.append(total_mask)
    return jnp.stack(collected).astype(jnp.int32)


def level_of(own_key, shape, shards, least, high):
    loudness = 1.0
    for dim, parts in shards:
        heights = jax.random.uniform(jax.random.fold_in(jax.random.fold_in(own_key, 6), dim), (parts,), jnp.float32, least / len(shards), high / len(shards))
        loudness = loudness * jnp.repeat(jnp.exp(heights), shape[dim] // parts).reshape((-1,) + (1,) * (len(shape) - 1 - dim))
    return loudness


def scatter_about(key, shape, scale, most, pieces=(), kind=jnp.bfloat16):
    drawn = jax.random.normal(key, shape, jnp.float32) * scale
    if len(pieces) > 0:
        drawn = level_of(key, shape, pieces, -0.22, 0.18) * drawn
    return jnp.clip(drawn, min=-most, max=most).astype(kind)


def setup_inputs(seed: int = 0) -> dict:
    key_of = jax.random.split(jax.random.key(seed), 4)
    return {
        "snapshots": scatter_about(key_of[0], (CELLS, SNAPS), 1.0, 6.0, ((0, 4), (1, 8))),
        "volume": jnp.clip(jnp.exp(math.log(4.0) - 2.7725887 * jax.random.uniform(key_of[1], (CELLS,), jnp.float32) ** level_of(key_of[1], (CELLS,), ((0, 4),), -0.2, 0.2)), 0.25, 4.0),
        "masks": draw_masks(jax.random.fold_in(key_of[3], 71), 0),
    }


def reference(snapshots, volume, masks):
    weighted = (snapshots.astype(jnp.float32) * jnp.sqrt(volume)[:, None]).astype(jnp.bfloat16)
    weighted_blocks = weighted.reshape(CELLS, GROUPS, GROUP).transpose(1, 0, 2)
    scale_factor = float(CELLS) ** (-0.5)
    group_index = jnp.arange(GROUPS, dtype=jnp.int32)
    results = []
    for round_number in range(ROUNDS):
        partners = jnp.bitwise_xor(group_index, masks[round_number]).astype(jnp.int32)

        def one_tile(pair):
            left_block = weighted_blocks[pair[0]]
            right_block = weighted_blocks[pair[1]]
            product = lax.dot_general(left_block, right_block, (((0,), (0,)), ((), ())), preferred_element_type=jnp.float32)
            return product * scale_factor
        results.append(lax.map(one_tile, (group_index, partners)))
    return jnp.stack(results)
```

```python
from functools import partial
from itertools import product

import jax
import jax.numpy as jnp
from jax import lax
from jax.sharding import PartitionSpec as P

ROUNDS = 4
PIECES = 2


def exchange(part, axis, mask):
    return lax.ppermute(part, axis, [(i, i ^ mask) for i in range(lax.axis_size(axis))])


def gram(left, right):
    total = None
    for one, other in zip(left, right):
        term = lax.dot_general(
            one, other, (((0,), (0,)), ((), ())), preferred_element_type=jnp.float32
        )
        total = term if total is None else total + term
    return total


def summed_block(tile, dimension):
    count = lax.axis_size("space")
    me = lax.axis_index("space")
    width = tile.shape[dimension] // count

    def block(index):
        return lax.dynamic_slice_in_dim(tile, index * width, width, dimension)

    arrived = [
        exchange(block(jnp.bitwise_xor(me, other)).astype(jnp.bfloat16), "space", other)
        for other in range(1, count)
    ]
    total = block(me)
    for part in arrived:
        total = total + part.astype(jnp.float32)
    return total


def chained(masks, pieces, scale_factor):
    bit_count = lax.axis_size("snap").bit_length() - 1
    weighted = jnp.concatenate(pieces)
    branches = [partial(exchange, axis="snap", mask=1 << position) for position in range(bit_count)]
    held, previous, results = weighted, jnp.int32(0), []
    for round_number in range(ROUNDS):
        delta = jnp.bitwise_xor(masks[round_number], previous)
        which_bit = jnp.int32(0)
        for position in range(bit_count):
            which_bit = which_bit + position * jnp.bitwise_and(jnp.right_shift(delta, position), 1)
        held = lax.switch(which_bit, branches, held)
        previous = masks[round_number]
        results.append(
            lax.psum_scatter(
                gram([weighted], [held]) * scale_factor, "space", scatter_dimension=0, tiled=True
            )
        )
    return jnp.stack(results)


def sequences(groups):
    found = [[1 << bit] for bit in range(groups.bit_length() - 1)]
    for _ in range(ROUNDS - 1):
        found = [
            masks + [masks[-1] ^ 1 << bit]
            for masks in found
            for bit in range(groups.bit_length() - 1)
            if masks[-1] ^ 1 << bit not in masks + [0]
        ]
    return found


def route(masks):
    inside = [mask for mask in masks if mask < 4]
    across = [mask & 3 for mask in masks if mask >= 4]
    best = None
    for own in product((0, 1, 2), repeat=3):
        for half in product((0, 1), repeat=3):
            for own_last, half_last in product((1, 2), repeat=2):
                own_of = dict(zip((0, 1, 2, 3), (2,) + own))
                half_of = dict(zip((0, 1, 2, 3), (1,) + half))
                if any(own_of[mask] < 2 for mask in inside):
                    continue
                if own_of[3] > own_of[3 ^ own_last] or half_of[3] > half_of[3 ^ half_last]:
                    continue
                pairs = []
                for mask in across:
                    able = [e for e in (0, 1, 2, 3) if own_of[e] and half_of[e ^ mask]]
                    if able:
                        pairs.append((able[0], able[0] ^ mask))
                if len(pairs) < len(across):
                    continue
                load = {1: 0, 2: 1}
                for bit in (1, 2):
                    load[bit] += own_of[bit] + half_of[bit]
                load[own_last] += own_of[3]
                load[half_last] += half_of[3]
                cost = (max(load.values()), sum(load.values()), -own_last)
                if best is None or cost < best[0]:
                    best = (cost, own_of, own_last, half_of, half_last, dict(zip(across, pairs)))
    return best[1:]


def planned(pieces, masks, scale_factor):
    own_of, own_last, half_of, half_last, pairs = route(masks)
    cut = lax.axis_size("snap") // 2
    half = PIECES
    kept, given = pieces[:half], pieces[half:]
    own = {0: list(pieces)}
    other = {0: [exchange(piece, "snap", cut) for piece in given]}
    for bit in (1, 2):
        if own_of[bit]:
            own[bit] = [exchange(piece, "snap", bit) for piece in pieces[: half * own_of[bit]]]
    if own_of[3]:
        source = own[3 ^ own_last]
        own[3] = [exchange(piece, "snap", own_last) for piece in source[: half * own_of[3]]]
    for bit in (1, 2):
        if half_of[bit]:
            other[bit] = [exchange(piece, "snap", bit) for piece in other[0]]
    if half_of[3]:
        other[3] = [exchange(piece, "snap", half_last) for piece in other[3 ^ half_last]]

    results = []
    for mask in masks:
        if mask < cut:
            results.append(summed_block(gram(own[0], own[mask]) * scale_factor, 0))
            continue
        mine, theirs = pairs[mask ^ cut]
        tile = gram(own[mine][:half], other[theirs]) * scale_factor
        rows = summed_block(tile, 0)
        if mine:
            rows = exchange(rows.astype(jnp.bfloat16), "snap", mine).astype(jnp.float32)
        columns = summed_block(tile, 1).T.astype(jnp.bfloat16)
        columns = exchange(columns, "snap", theirs ^ cut).astype(jnp.float32)
        results.append(rows + columns)
    return jnp.stack(results)


def body(snapshots, volume, masks):
    slab_count = lax.axis_size("space")
    groups = lax.axis_size("snap")
    cells = snapshots.shape[0]
    scale_factor = float(cells * slab_count) ** (-0.5)
    roots = jnp.sqrt(volume)[:, None]
    upper = (lax.axis_index("snap") >= groups // 2).astype(jnp.int32)
    count = 2 * PIECES
    size = cells // count
    pieces = []
    for number in range(count):
        start = jnp.where(upper == 1, (number + PIECES) % count, number) * size
        part = lax.dynamic_slice_in_dim(snapshots, start, size)
        scale = lax.dynamic_slice_in_dim(roots, start, size)
        pieces.append((part.astype(jnp.float32) * scale).astype(jnp.bfloat16))
    if groups == 8:
        allowed = sequences(groups)
        which = jnp.int32(0)
        for number, sequence in enumerate(allowed):
            same = jnp.all(masks == jnp.array(sequence, jnp.int32))
            which = which + number * same.astype(jnp.int32)
        branches = [
            partial(planned, masks=sequence, scale_factor=scale_factor) for sequence in allowed
        ]
        stacked = lax.switch(which, branches, pieces)
    else:
        stacked = chained(masks, pieces, scale_factor)
    return stacked[:, None]


def solution(mesh):
    in_specs = (P("space", "snap"), P("space"), P())
    out_specs = P(None, "snap", "space", None)
    return jax.shard_map(body, mesh=mesh, in_specs=in_specs, out_specs=out_specs, check_vma=False)
```

```python
import jax
import jax.numpy as jnp
from jax import lax
from jax.experimental import pallas as pl
from jax.experimental.pallas import tpu as pltpu
from jax.sharding import PartitionSpec as P

ROUNDS = 4
OWN_PIECES = 2
MATE_PIECES = 2


def exchange(part, axis, mask):
    return lax.ppermute(part, axis, [(i, i ^ mask) for i in range(lax.axis_size(axis))])


def products(choices, lefts, blocks, scale_factor):
    slab_count = lax.axis_size("space")
    group, cells = lefts.shape[1:]
    width = blocks[0].shape[1]
    rows = group // slab_count

    def kernel(choices_ref, lefts_ref, *refs):
        block_refs = refs[: len(blocks)]
        out_refs = refs[len(blocks) : len(blocks) + slab_count]
        picked, tile = refs[len(blocks) + slab_count :]

        def one_round(round_number, carry):
            for number, block_ref in enumerate(block_refs):

                @pl.when(choices_ref[round_number] == number)
                def _():
                    picked[...] = block_ref[...]

            left = lefts_ref[choices_ref[ROUNDS + round_number]]
            tile[...] = scale_factor * jnp.dot(
                left, picked[...], preferred_element_type=jnp.float32
            )
            for number, out_ref in enumerate(out_refs):
                start = jnp.bitwise_xor(choices_ref[2 * ROUNDS], number) * rows
                part = tile[pl.ds(pl.multiple_of(start, rows), rows), :]
                out_ref[round_number] = part.astype(out_ref.dtype)
            return carry

        lax.fori_loop(0, ROUNDS, one_round, 0)

    vmem = pl.BlockSpec(memory_space=pltpu.VMEM)
    return pl.pallas_call(
        kernel,
        out_shape=[
            jax.ShapeDtypeStruct((ROUNDS, rows, width), jnp.bfloat16 if number else jnp.float32)
            for number in range(slab_count)
        ],
        in_specs=[pl.BlockSpec(memory_space=pltpu.SMEM)] + [vmem] * (1 + len(blocks)),
        out_specs=[vmem] * slab_count,
        scratch_shapes=[
            pltpu.VMEM((cells, width), jnp.bfloat16),
            pltpu.VMEM((group, width), jnp.float32),
        ],
        compiler_params=pltpu.CompilerParams(vmem_limit_bytes=32 * 2**20),
        cost_estimate=pl.CostEstimate(
            flops=2 * ROUNDS * group * cells * width,
            bytes_accessed=2 * (lefts.size + len(blocks) * cells * width + ROUNDS * group * width),
            transcendentals=0,
        ),
    )(choices, lefts, *blocks)


def summed(parts):
    total = parts[0]
    for other in range(1, len(parts)):
        total = total + exchange(parts[other], "space", other).astype(jnp.float32)
    return total


def gathered(piece, cut):
    held = {0: piece}
    bit = cut // 2
    while bit:
        for low, block in list(held.items()):
            held[low | bit] = exchange(block, "snap", bit)
        bit //= 2
    return [held[low] for low in range(cut)]


def body(snapshots, volume, masks):
    slab_count = lax.axis_size("space")
    cut = lax.axis_size("snap") // 2
    cells, group = snapshots.shape
    scale_factor = float(cells * slab_count) ** (-0.5)
    half = cells // 2
    upper = (lax.axis_index("snap") >= cut).astype(jnp.int32)
    roots = jnp.sqrt(volume)[:, None]

    def weighted(side, first, count):
        part = lax.dynamic_slice(snapshots, (side * half, first), (half, count))
        scale = lax.dynamic_slice_in_dim(roots, side * half, half)
        return (part.astype(jnp.float32) * scale).astype(jnp.bfloat16)

    def pieces_of(side, count):
        width = group // count
        return [weighted(side, number * width, width) for number in range(count)]

    mate = [exchange(piece, "snap", cut) for piece in pieces_of(1 - upper, MATE_PIECES)]
    own = pieces_of(upper, OWN_PIECES)
    lefts = jnp.stack([weighted(upper, 0, group).T, jnp.concatenate(mate, axis=1).T])

    low = jnp.bitwise_and(masks, cut - 1)
    crossing = (masks >= cut).astype(jnp.int32)
    me = lax.axis_index("space").astype(jnp.int32)[None]
    own_choices = jnp.concatenate([low, crossing, me])
    mate_choices = jnp.concatenate([low, 1 - crossing, me])

    own_sums = [
        summed(products(own_choices, lefts, gathered(piece, cut), scale_factor)) for piece in own
    ]
    own_sum = jnp.concatenate(own_sums, axis=2)
    swap = (crossing == 1)[:, None, None]
    columns = []
    for number, piece in enumerate(mate):
        mate_sum = summed(products(mate_choices, lefts, gathered(piece, cut), scale_factor))
        width = group // MATE_PIECES
        held = lax.slice_in_dim(own_sum, number * width, (number + 1) * width, axis=2)
        keep = jnp.where(swap, mate_sum, held)
        give = jnp.where(swap, held, mate_sum).astype(jnp.bfloat16)
        columns.append(keep + exchange(give, "snap", cut).astype(jnp.float32))
    return jnp.concatenate(columns, axis=2)[:, None]


def solution(mesh):
    in_specs = (P("space", "snap"), P("space"), P())
    out_specs = P(None, "snap", "space", None)
    return jax.shard_map(body, mesh=mesh, in_specs=in_specs, out_specs=out_specs, check_vma=False)
```

```python
import jax
import jax.numpy as jnp
from jax import lax
from jax.experimental import pallas as pl
from jax.experimental.pallas import tpu as pltpu
from jax.sharding import PartitionSpec as P

ROUNDS = 4
PIECES = 2
VMEM = pl.BlockSpec(memory_space=pltpu.VMEM)
PARAMS = pltpu.CompilerParams(vmem_limit_bytes=40 * 2**20)


def exchange(part, axis, mask):
    return lax.ppermute(part, axis, [(i, i ^ mask) for i in range(lax.axis_size(axis))])


def turned(own, mate):
    cells, width = own[0].shape
    group = width * len(own)

    def kernel(*refs):
        out_ref = refs[-1]
        for number, ref in enumerate(refs[:-1]):
            which, place = divmod(number, len(own))
            out_ref[which, place * width : (place + 1) * width, :] = ref[...].T

    return pl.pallas_call(
        kernel,
        out_shape=jax.ShapeDtypeStruct((2, group, cells), own[0].dtype),
        in_specs=[VMEM] * (2 * len(own)),
        out_specs=VMEM,
        compiler_params=PARAMS,
        cost_estimate=pl.CostEstimate(
            flops=0, bytes_accessed=8 * group * cells, transcendentals=0
        ),
    )(*own, *mate)


def products(choices, lefts, blocks, scale_factor):
    slab_count = lax.axis_size("space")
    group, cells = lefts.shape[1:]
    width = blocks.shape[2]
    rows = group // slab_count

    def kernel(choices_ref, lefts_ref, blocks_ref, even_ref, odd_ref, tile):
        def one_round(round_number, carry):
            left = lefts_ref[choices_ref[ROUNDS + round_number]]
            right = blocks_ref[choices_ref[round_number]]
            tile[...] = scale_factor * jnp.dot(left, right, preferred_element_type=jnp.float32)
            for number in range(slab_count):
                start = jnp.bitwise_xor(choices_ref[2 * ROUNDS], number) * rows
                part = tile[pl.ds(pl.multiple_of(start, rows), rows), :]
                out_ref = odd_ref if number % 2 else even_ref
                out_ref[number // 2, round_number] = part.astype(out_ref.dtype)
            return carry

        lax.fori_loop(0, ROUNDS, one_round, 0)

    shape = (slab_count // 2, ROUNDS, rows, width)
    return pl.pallas_call(
        kernel,
        out_shape=[jax.ShapeDtypeStruct(shape, kind) for kind in (jnp.float32, jnp.bfloat16)],
        in_specs=[pl.BlockSpec(memory_space=pltpu.SMEM), VMEM, VMEM],
        out_specs=[VMEM, VMEM],
        scratch_shapes=[pltpu.VMEM((group, width), jnp.float32)],
        compiler_params=PARAMS,
        cost_estimate=pl.CostEstimate(
            flops=2 * ROUNDS * group * cells * width,
            bytes_accessed=2 * (lefts.size + blocks.size + 2 * ROUNDS * group * width),
            transcendentals=0,
        ),
    )(choices, lefts, blocks)


def summed(keep, send):
    bit = 1
    while True:
        total = keep + exchange(send, "space", bit).astype(jnp.float32)
        if len(total) == 1:
            return total[0]
        keep, send = total[0::2], total[1::2].astype(jnp.bfloat16)
        bit *= 2


def body(snapshots, volume, masks):
    slab_count = lax.axis_size("space")
    groups = lax.axis_size("snap")
    cut = groups // 2
    cells, group = snapshots.shape
    width = group // PIECES
    scale_factor = float(cells * slab_count) ** (-0.5)
    half = cells // 2
    place = lax.axis_index("snap").astype(jnp.int32)
    upper = (place >= cut).astype(jnp.int32)
    roots = jnp.sqrt(volume)[:, None]
    sides = [list(range(cut)), list(range(cut, groups))]

    def pieces_of(side):
        scale = lax.dynamic_slice_in_dim(roots, side * half, half)
        found = []
        for number in range(PIECES):
            part = lax.dynamic_slice(snapshots, (side * half, number * width), (half, width))
            found.append((part.astype(jnp.float32) * scale).astype(jnp.bfloat16))
        return found

    def gathered(piece):
        return lax.all_gather(piece, "snap", axis_index_groups=sides)

    mate = [exchange(piece, "snap", cut) for piece in pieces_of(1 - upper)]
    own = pieces_of(upper)
    lefts = turned(own, mate)

    low = jnp.bitwise_and(jnp.bitwise_xor(masks, place), cut - 1)
    crossing = (masks >= cut).astype(jnp.int32)
    me = lax.axis_index("space").astype(jnp.int32)[None]
    own_choices = jnp.concatenate([low, crossing, me])
    mate_choices = jnp.concatenate([low, 1 - crossing, me])

    own_sums = [summed(*products(own_choices, lefts, gathered(piece), scale_factor)) for piece in own]
    swap = (crossing == 1)[:, None, None]
    columns = []
    for held, piece in zip(own_sums, mate):
        mate_sum = summed(*products(mate_choices, lefts, gathered(piece), scale_factor))
        keep = jnp.where(swap, mate_sum, held)
        give = jnp.where(swap, held, mate_sum).astype(jnp.bfloat16)
        columns.append(keep + exchange(give, "snap", cut).astype(jnp.float32))
    return jnp.concatenate(columns, axis=2)[:, None]


def solution(mesh):
    in_specs = (P("space", "snap"), P("space"), P())
    out_specs = P(None, "snap", "space", None)
    return jax.shard_map(body, mesh=mesh, in_specs=in_specs, out_specs=out_specs, check_vma=False)
```

```python
import jax
import jax.numpy as jnp
from jax import lax
from jax.experimental import pallas as pl
from jax.experimental.pallas import tpu as pltpu
from jax.sharding import PartitionSpec as P

ROUNDS = 4
OWN_WIDTHS = (2, 2)
MATE_WIDTHS = (2, 1, 1)
NEAR_FIRST = (3,)
VMEM = pl.BlockSpec(memory_space=pltpu.VMEM)
PARAMS = pltpu.CompilerParams(vmem_limit_bytes=40 * 2**20)


def exchange(part, axis, mask):
    return lax.ppermute(part, axis, [(i, i ^ mask) for i in range(lax.axis_size(axis))])


def behind(value, earlier):
    return value if earlier is None else lax.optimization_barrier((value, earlier))[0]


def hops_in_order(widths, cut):
    waiting = []
    for piece in range(len(widths)):
        bits, held = [1 << n for n in range(cut.bit_length() - 1)], [0]
        for bit in bits if piece in NEAR_FIRST else reversed(bits):
            waiting += [(piece, low, bit) for low in held]
            held += [low | bit for low in held]
    ready, crossed = {}, 0
    for piece, width in enumerate(widths):
        crossed += 2 * width if piece >= len(OWN_WIDTHS) else 0
        ready[piece, 0] = crossed
    free, ordered = {}, []
    while waiting:
        def start_of(hop):
            return max(free.get(hop[2], 0), ready[hop[:2]])

        able = [hop for hop in waiting if hop[:2] in ready]
        hop = min(able, key=lambda one: (start_of(one), waiting.index(one)))
        piece, low, bit = hop
        shared = 2 if bit == cut // 2 and start_of(hop) < crossed else 1
        free[bit] = ready[piece, low | bit] = start_of(hop) + shared * widths[piece]
        waiting.remove(hop)
        ordered.append(hop)
    return ordered


def gathered(pieces, widths, cut):
    held = [{0: piece} for piece in pieces]
    behind_of = {}
    for piece, low, bit in hops_in_order(widths, cut):
        earlier = behind_of.setdefault(bit, [])
        depth = 2 if bit == 1 else 1
        block = behind(held[piece][low], earlier[-depth] if len(earlier) >= depth else None)
        held[piece][low | bit] = exchange(block, "snap", bit)
        earlier.append(held[piece][low | bit])
    return [[found[low] for low in range(cut)] for found in held]


def turned(own, mate):
    cells = own[0].shape[0]
    group = sum(piece.shape[1] for piece in own)

    def kernel(*refs):
        out_ref = refs[-1]
        for which, some in enumerate((refs[: len(own)], refs[len(own) : -1])):
            first = 0
            for ref in some:
                out_ref[which, first : first + ref.shape[1], :] = ref[...].T
                first += ref.shape[1]

    return pl.pallas_call(
        kernel,
        out_shape=jax.ShapeDtypeStruct((2, group, cells), own[0].dtype),
        in_specs=[VMEM] * (len(own) + len(mate)),
        out_specs=VMEM,
        compiler_params=PARAMS,
        cost_estimate=pl.CostEstimate(
            flops=0, bytes_accessed=8 * group * cells, transcendentals=0
        ),
    )(*own, *mate)


def products(choices, lefts, blocks, scale_factor):
    slab_count = lax.axis_size("space")
    group, cells = lefts.shape[1:]
    width = blocks[0].shape[1]
    rows = group // slab_count

    def kernel(choices_ref, lefts_ref, *refs):
        block_refs = refs[: len(blocks)]
        even_ref, odd_ref, picked, tile = refs[len(blocks) :]

        def one_round(round_number, carry):
            for number, block_ref in enumerate(block_refs):

                @pl.when(choices_ref[round_number] == number)
                def _():
                    picked[...] = block_ref[...]

            left = lefts_ref[choices_ref[ROUNDS + round_number]]
            tile[...] = scale_factor * jnp.dot(
                left, picked[...], preferred_element_type=jnp.float32
            )
            for number in range(slab_count):
                start = jnp.bitwise_xor(choices_ref[2 * ROUNDS], number) * rows
                part = tile[pl.ds(pl.multiple_of(start, rows), rows), :]
                out_ref = odd_ref if number % 2 else even_ref
                out_ref[number // 2, round_number] = part.astype(out_ref.dtype)
            return carry

        lax.fori_loop(0, ROUNDS, one_round, 0)

    shape = (slab_count // 2, ROUNDS, rows, width)
    return pl.pallas_call(
        kernel,
        out_shape=[jax.ShapeDtypeStruct(shape, kind) for kind in (jnp.float32, jnp.bfloat16)],
        in_specs=[pl.BlockSpec(memory_space=pltpu.SMEM)] + [VMEM] * (1 + len(blocks)),
        out_specs=[VMEM, VMEM],
        scratch_shapes=[
            pltpu.VMEM((cells, width), jnp.bfloat16),
            pltpu.VMEM((group, width), jnp.float32),
        ],
        compiler_params=PARAMS,
        cost_estimate=pl.CostEstimate(
            flops=2 * ROUNDS * group * cells * width,
            bytes_accessed=2 * (lefts.size + (len(blocks) * cells + 2 * ROUNDS * group) * width),
            transcendentals=0,
        ),
    )(choices, lefts, *blocks)


def summed(keep, send):
    bit = 1
    while True:
        total = keep + exchange(send, "space", bit).astype(jnp.float32)
        if len(total) == 1:
            return total[0]
        keep, send = total[0::2], total[1::2].astype(jnp.bfloat16)
        bit *= 2


def body(snapshots, volume, masks):
    slab_count = lax.axis_size("space")
    groups = lax.axis_size("snap")
    cut = groups // 2
    cells, group = snapshots.shape
    quarter = group // 4
    scale_factor = float(cells * slab_count) ** (-0.5)
    half = cells // 2
    place = lax.axis_index("snap").astype(jnp.int32)
    upper = (place >= cut).astype(jnp.int32)
    roots = jnp.sqrt(volume)[:, None]

    def pieces_of(side, widths):
        scale = lax.dynamic_slice_in_dim(roots, side * half, half)
        found, first = [], 0
        for width in widths:
            part = lax.dynamic_slice(
                snapshots, (side * half, first * quarter), (half, width * quarter)
            )
            found.append((part.astype(jnp.float32) * scale).astype(jnp.bfloat16))
            first += width
        return found

    mate, crossed = [], None
    for piece in pieces_of(1 - upper, MATE_WIDTHS):
        crossed = exchange(behind(piece, crossed), "snap", cut)
        mate.append(crossed)
    own = pieces_of(upper, OWN_WIDTHS)
    lefts = turned(own, mate)
    blocks = gathered(own + mate, OWN_WIDTHS + MATE_WIDTHS, cut)

    low = jnp.bitwise_and(masks, cut - 1)
    crossing = (masks >= cut).astype(jnp.int32)
    me = lax.axis_index("space").astype(jnp.int32)[None]
    own_choices = jnp.concatenate([low, crossing, me])
    mate_choices = jnp.concatenate([low, 1 - crossing, me])

    own_sum = jnp.concatenate(
        [
            summed(*products(own_choices, lefts, found, scale_factor))
            for found in blocks[: len(own)]
        ],
        axis=2,
    )
    swap = (crossing == 1)[:, None, None]
    columns, first = [], 0
    for found in blocks[len(own) :]:
        mate_sum = summed(*products(mate_choices, lefts, found, scale_factor))
        held = lax.slice_in_dim(own_sum, first, first + mate_sum.shape[2], axis=2)
        keep = jnp.where(swap, mate_sum, held)
        give = jnp.where(swap, held, mate_sum).astype(jnp.bfloat16)
        columns.append(keep + exchange(give, "snap", cut).astype(jnp.float32))
        first += mate_sum.shape[2]
    return jnp.concatenate(columns, axis=2)[:, None]


def solution(mesh):
    in_specs = (P("space", "snap"), P("space"), P())
    out_specs = P(None, "snap", "space", None)
    return jax.shard_map(body, mesh=mesh, in_specs=in_specs, out_specs=out_specs, check_vma=False)
```

```python
import jax
import jax.numpy as jnp
from jax import lax
from jax.experimental import pallas as pl
from jax.experimental.pallas import tpu as pltpu
from jax.sharding import PartitionSpec as P

ROUNDS = 4
OWN_WIDTHS = (2, 2)
CROSSING_WIDTHS = (2, 2)
MATE_WIDTHS = (2, 1, 1)
NEAR_FIRST = (3,)
URGENCY = (0, 2, 1, 3, 4)
BATCHES = (((0,), (2,)), ((1,),), ((3, 4),))
VMEM = pl.BlockSpec(memory_space=pltpu.VMEM)
PARAMS = pltpu.CompilerParams(vmem_limit_bytes=40 * 2**20)


def exchange(part, axis, mask):
    return lax.ppermute(part, axis, [(i, i ^ mask) for i in range(lax.axis_size(axis))])


def behind(value, earlier):
    return value if earlier is None else lax.optimization_barrier((value, earlier))[0]


def hops_in_order(widths, cut):
    waiting = []
    for piece in URGENCY:
        bits, held = [1 << n for n in range(cut.bit_length() - 1)], [0]
        for bit in bits if piece in NEAR_FIRST else reversed(bits):
            waiting += [(piece, low, bit) for low in held]
            held += [low | bit for low in held]
    ready, crossed = {}, 0
    for piece, width in enumerate(widths):
        crossed += 2 * width if piece >= len(OWN_WIDTHS) else 0
        ready[piece, 0] = crossed
    free, ordered = {}, []
    while waiting:
        def start_of(hop):
            return max(free.get(hop[2], 0), ready[hop[:2]])

        able = [hop for hop in waiting if hop[:2] in ready]
        hop = min(able, key=lambda one: (start_of(one), waiting.index(one)))
        piece, low, bit = hop
        shared = 2 if bit == cut // 2 and start_of(hop) < crossed else 1
        free[bit] = ready[piece, low | bit] = start_of(hop) + shared * widths[piece]
        waiting.remove(hop)
        ordered.append(hop)
    return ordered


def turned(own, mate):
    cells = own[0].shape[0]
    group = sum(piece.shape[1] for piece in own)

    def kernel(*refs):
        out_ref = refs[-1]
        for which, some in enumerate((refs[: len(own)], refs[len(own) : -1])):
            first = 0
            for ref in some:
                out_ref[which, first : first + ref.shape[1], :] = ref[...].T
                first += ref.shape[1]

    return pl.pallas_call(
        kernel,
        out_shape=jax.ShapeDtypeStruct((2, group, cells), own[0].dtype),
        in_specs=[VMEM] * (len(own) + len(mate)),
        out_specs=VMEM,
        compiler_params=PARAMS,
        cost_estimate=pl.CostEstimate(
            flops=0, bytes_accessed=8 * group * cells, transcendentals=0
        ),
    )(*own, *mate)


def products(choices, lefts, batch, scale_factor):
    slab_count = lax.axis_size("space")
    group, cells = lefts.shape[1:]
    widths = [sum(blocks[0].shape[1] for blocks in pieces) for _, pieces in batch]
    rows = group // slab_count
    arrays = [block for _, pieces in batch for blocks in pieces for block in blocks]

    def kernel(choices_ref, lefts_ref, *refs):
        waiting = list(refs[: len(arrays)])
        even_ref, odd_ref, picked, tile = refs[len(arrays) :]
        first = 0
        for (mates, pieces), width in zip(batch, widths):
            sources = [[waiting.pop(0) for _ in blocks] for blocks in pieces]
            columns = pl.ds(first, width)
            first += width

            def one_round(round_number, carry):
                begin = 0
                for block_refs in sources:
                    end = begin + block_refs[0].shape[1]
                    for number, block_ref in enumerate(block_refs):

                        @pl.when(choices_ref[round_number] == number)
                        def _():
                            picked[:, begin:end] = block_ref[...]

                    begin = end
                side = choices_ref[ROUNDS + round_number]
                left = lefts_ref[1 - side if mates else side]
                tile[:, :width] = scale_factor * jnp.dot(
                    left, picked[:, :width], preferred_element_type=jnp.float32
                )
                for number in range(slab_count):
                    start = jnp.bitwise_xor(choices_ref[2 * ROUNDS], number) * rows
                    part = tile[pl.ds(pl.multiple_of(start, rows), rows), :width]
                    out_ref = odd_ref if number % 2 else even_ref
                    out_ref[number // 2, round_number, :, columns] = part.astype(out_ref.dtype)
                return carry

            lax.fori_loop(0, ROUNDS, one_round, 0)

    shape = (slab_count // 2, ROUNDS, rows, sum(widths))
    return pl.pallas_call(
        kernel,
        out_shape=[jax.ShapeDtypeStruct(shape, kind) for kind in (jnp.float32, jnp.bfloat16)],
        in_specs=[pl.BlockSpec(memory_space=pltpu.SMEM)] + [VMEM] * (1 + len(arrays)),
        out_specs=[VMEM, VMEM],
        scratch_shapes=[
            pltpu.VMEM((cells, max(widths)), jnp.bfloat16),
            pltpu.VMEM((group, max(widths)), jnp.float32),
        ],
        compiler_params=PARAMS,
        cost_estimate=pl.CostEstimate(
            flops=2 * ROUNDS * group * cells * sum(widths),
            bytes_accessed=2 * lefts.size
            + 2 * sum(array.size for array in arrays)
            + 4 * ROUNDS * group * sum(widths),
            transcendentals=0,
        ),
    )(choices, lefts, *arrays)


def halved(keep, send, bit):
    return keep + exchange(send, "space", bit).astype(jnp.float32)


def summed(total):
    bit = 2
    while len(total) > 1:
        total = halved(total[0::2], total[1::2].astype(jnp.bfloat16), bit)
        bit *= 2
    return total[0]


def body(snapshots, volume, masks):
    slab_count = lax.axis_size("space")
    groups = lax.axis_size("snap")
    cut = groups // 2
    cells, group = snapshots.shape
    quarter = group // 4
    scale_factor = float(cells * slab_count) ** (-0.5)
    half = cells // 2
    place = lax.axis_index("snap").astype(jnp.int32)
    upper = (place >= cut).astype(jnp.int32)
    roots = jnp.sqrt(volume)[:, None]

    def pieces_of(side, widths):
        scale = lax.dynamic_slice_in_dim(roots, side * half, half)
        found, first = [], 0
        for width in widths:
            part = lax.dynamic_slice(
                snapshots, (side * half, first * quarter), (half, width * quarter)
            )
            found.append((part.astype(jnp.float32) * scale).astype(jnp.bfloat16))
            first += width
        return found

    crossed = []
    for piece in pieces_of(1 - upper, CROSSING_WIDTHS):
        crossed.append(exchange(behind(piece, crossed[-1] if crossed else None), "snap", cut))
    own = pieces_of(upper, OWN_WIDTHS)
    lefts = turned(own, crossed)
    mate = []
    for width in MATE_WIDTHS:
        first = sum(piece.shape[1] for piece in mate)
        for piece in crossed:
            if first < piece.shape[1]:
                break
            first -= piece.shape[1]
        mate.append(lax.slice_in_dim(piece, first, first + width * quarter, axis=1))

    low = jnp.bitwise_and(masks, cut - 1)
    crossing = (masks >= cut).astype(jnp.int32)
    me = lax.axis_index("space").astype(jnp.int32)[None]
    choices = jnp.concatenate([low, crossing, me])
    swap = (crossing == 1)[:, None, None]

    held = [{0: piece} for piece in own + mate]
    sent = {}
    halves, given, sums, columns, back = [], [], {}, [], []

    def add_batch():
        lists = BATCHES[len(halves)]
        batch = [
            (numbers[0] >= len(own), [[held[n][low] for low in range(cut)] for n in numbers])
            for numbers in lists
        ]
        earlier = (given[0], halves[-1]) if lists == BATCHES[-1] else None
        even, odd = products(behind(choices, earlier), lefts, batch, scale_factor)
        halves.append(halved(even, odd, 1))
        total = summed(halves[-1])
        taken = 0
        for (mates, pieces), numbers in zip(batch, lists):
            width = sum(found[0].shape[1] for found in pieces)
            part = lax.slice_in_dim(total, taken, taken + width, axis=2)
            taken += width
            if not mates:
                sums[numbers[0]] = part
                continue
            own_part = sums[len(columns)]
            keep = jnp.where(swap, part, own_part)
            given.append(jnp.where(swap, own_part, part).astype(jnp.bfloat16))
            back.append(exchange(behind(given[-1], back[-1] if back else None), "snap", cut))
            columns.append(keep + back[-1].astype(jnp.float32))

    for piece, low, bit in hops_in_order(OWN_WIDTHS + MATE_WIDTHS, cut):
        earlier = sent.setdefault(bit, [])
        depth = 2 if bit == 1 else 1
        ties = earlier[-depth] if len(earlier) >= depth else None
        held[piece][low | bit] = exchange(behind(held[piece][low], ties), "snap", bit)
        earlier.append(held[piece][low | bit])
        while len(halves) < len(BATCHES) and all(
            len(held[n]) == cut for numbers in BATCHES[len(halves)] for n in numbers
        ):
            add_batch()
    return jnp.concatenate(columns, axis=2)[:, None]


def solution(mesh):
    in_specs = (P("space", "snap"), P("space"), P())
    out_specs = P(None, "snap", "space", None)
    return jax.shard_map(body, mesh=mesh, in_specs=in_specs, out_specs=out_specs, check_vma=False)
```

```python
import jax
import jax.numpy as jnp
from jax import lax
from jax.experimental import pallas as pl
from jax.experimental.pallas import tpu as pltpu
from jax.sharding import PartitionSpec as P

ROUNDS = 4
OWN_WIDTHS = (2, 2)
CROSSING_WIDTHS = (2, 2)
MATE_WIDTHS = (2, 1, 1)
NEAR_FIRST = (3,)
URGENCY = (0, 2, 1, 3, 4)
BATCHES = (((0,), (2,)), ((1,),), ((3, 4),))
VMEM = pl.BlockSpec(memory_space=pltpu.VMEM)
PARAMS = pltpu.CompilerParams(vmem_limit_bytes=40 * 2**20)


def exchange(part, axis, mask):
    return lax.ppermute(part, axis, [(i, i ^ mask) for i in range(lax.axis_size(axis))])


def behind(value, earlier):
    return value if earlier is None else lax.optimization_barrier((value, earlier))[0]


def hops_in_order(widths, cut):
    waiting = []
    for piece in URGENCY:
        bits, held = [1 << n for n in range(cut.bit_length() - 1)], [0]
        for bit in bits if piece in NEAR_FIRST else reversed(bits):
            waiting += [(piece, low, bit) for low in held]
            held += [low | bit for low in held]
    ready, crossed = {}, 0
    for piece, width in enumerate(widths):
        crossed += 2 * width if piece >= len(OWN_WIDTHS) else 0
        ready[piece, 0] = crossed
    free, ordered = {}, []
    while waiting:
        def start_of(hop):
            return max(free.get(hop[2], 0), ready[hop[:2]])

        able = [hop for hop in waiting if hop[:2] in ready]
        hop = min(able, key=lambda one: (start_of(one), -one[2], waiting.index(one)))
        piece, low, bit = hop
        shared = 2 if bit == cut // 2 and start_of(hop) < crossed else 1
        free[bit] = start_of(hop) + shared * widths[piece]
        ready[piece, low | bit] = free[bit] + 0.5
        waiting.remove(hop)
        ordered.append(hop)
    return ordered


def turned(own, mate):
    cells = own[0].shape[0]
    group = sum(piece.shape[1] for piece in own)

    def kernel(*refs):
        out_ref = refs[-1]
        for which, some in enumerate((refs[: len(own)], refs[len(own) : -1])):
            first = 0
            for ref in some:
                out_ref[which, first : first + ref.shape[1], :] = ref[...].T
                first += ref.shape[1]

    return pl.pallas_call(
        kernel,
        out_shape=jax.ShapeDtypeStruct((2, group, cells), own[0].dtype),
        in_specs=[VMEM] * (len(own) + len(mate)),
        out_specs=VMEM,
        compiler_params=PARAMS,
        cost_estimate=pl.CostEstimate(flops=0, bytes_accessed=0, transcendentals=0),
    )(*own, *mate)


def products(choices, lefts, batch, scale_factor):
    slab_count = lax.axis_size("space")
    group, cells = lefts.shape[1:]
    widths = [sum(blocks[0].shape[1] for blocks in pieces) for _, pieces in batch]
    rows = group // slab_count
    arrays = [block for _, pieces in batch for blocks in pieces for block in blocks]

    def kernel(choices_ref, lefts_ref, *refs):
        waiting = list(refs[: len(arrays)])
        even_ref, odd_ref, picked, tile = refs[len(arrays) :]
        first = 0
        for (mates, pieces), width in zip(batch, widths):
            sources = [[waiting.pop(0) for _ in blocks] for blocks in pieces]
            columns = pl.ds(first, width)
            first += width

            def one_round(round_number, carry):
                begin = 0
                for block_refs in sources:
                    end = begin + block_refs[0].shape[1]
                    for number, block_ref in enumerate(block_refs):

                        @pl.when(choices_ref[round_number] == number)
                        def _():
                            picked[:, begin:end] = block_ref[...]

                    begin = end
                side = choices_ref[ROUNDS + round_number]
                left = lefts_ref[1 - side if mates else side]
                tile[:, :width] = scale_factor * jnp.dot(
                    left, picked[:, :width], preferred_element_type=jnp.float32
                )
                for number in range(slab_count):
                    start = jnp.bitwise_xor(choices_ref[2 * ROUNDS], number) * rows
                    part = tile[pl.ds(pl.multiple_of(start, rows), rows), :width]
                    out_ref = odd_ref if number % 2 else even_ref
                    out_ref[number // 2, round_number, :, columns] = part.astype(out_ref.dtype)
                return carry

            lax.fori_loop(0, ROUNDS, one_round, 0)

    shape = (slab_count // 2, ROUNDS, rows, sum(widths))
    return pl.pallas_call(
        kernel,
        out_shape=[jax.ShapeDtypeStruct(shape, kind) for kind in (jnp.float32, jnp.bfloat16)],
        in_specs=[pl.BlockSpec(memory_space=pltpu.SMEM)] + [VMEM] * (1 + len(arrays)),
        out_specs=[VMEM, VMEM],
        scratch_shapes=[
            pltpu.VMEM((cells, max(widths)), jnp.bfloat16),
            pltpu.VMEM((group, max(widths)), jnp.float32),
        ],
        compiler_params=PARAMS,
        cost_estimate=pl.CostEstimate(flops=0, bytes_accessed=0, transcendentals=0),
    )(choices, lefts, *arrays)


def halved(keep, send, bit):
    return keep + exchange(send, "space", bit).astype(jnp.float32)


def summed(total):
    bit = 2
    while len(total) > 1:
        total = halved(total[0::2], total[1::2].astype(jnp.bfloat16), bit)
        bit *= 2
    return total[0]


def body(snapshots, volume, masks):
    slab_count = lax.axis_size("space")
    groups = lax.axis_size("snap")
    cut = groups // 2
    cells, group = snapshots.shape
    quarter = group // 4
    scale_factor = float(cells * slab_count) ** (-0.5)
    half = cells // 2
    place = lax.axis_index("snap").astype(jnp.int32)
    upper = (place >= cut).astype(jnp.int32)
    roots = jnp.sqrt(volume)[:, None]

    def pieces_of(side, widths):
        scale = lax.dynamic_slice_in_dim(roots, side * half, half)
        found, first = [], 0
        for width in widths:
            part = lax.dynamic_slice(
                snapshots, (side * half, first * quarter), (half, width * quarter)
            )
            found.append((part.astype(jnp.float32) * scale).astype(jnp.bfloat16))
            first += width
        return found

    crossed = []
    for piece in pieces_of(1 - upper, CROSSING_WIDTHS):
        crossed.append(exchange(behind(piece, crossed[-1] if crossed else None), "snap", cut))
    own = pieces_of(upper, OWN_WIDTHS)
    lefts = turned(own, crossed)
    mate = []
    for width in MATE_WIDTHS:
        first = sum(piece.shape[1] for piece in mate)
        for piece in crossed:
            if first < piece.shape[1]:
                break
            first -= piece.shape[1]
        mate.append(lax.slice_in_dim(piece, first, first + width * quarter, axis=1))

    low = jnp.bitwise_and(masks, cut - 1)
    crossing = (masks >= cut).astype(jnp.int32)
    me = lax.axis_index("space").astype(jnp.int32)[None]
    choices = jnp.concatenate([low, crossing, me])
    swap = (crossing == 1)[:, None, None]

    held = [{0: piece} for piece in own + mate]
    sent = {}
    halves, given, sums, columns, back = [], [], {}, [], []

    def add_batch():
        lists = BATCHES[len(halves)]
        batch = [
            (numbers[0] >= len(own), [[held[n][low] for low in range(cut)] for n in numbers])
            for numbers in lists
        ]
        earlier = None
        if not halves:
            earlier = (sent[cut // 2][-1], sent[1][4])
        elif lists != BATCHES[-1]:
            earlier = halves[0]
        else:
            earlier = (given[0], halves[-1])
        even, odd = products(behind(choices, earlier), lefts, batch, scale_factor)
        halves.append(halved(even, odd, 1))
        total = summed(halves[-1])
        taken = 0
        for (mates, pieces), numbers in zip(batch, lists):
            width = sum(found[0].shape[1] for found in pieces)
            part = lax.slice_in_dim(total, taken, taken + width, axis=2)
            taken += width
            if not mates:
                sums[numbers[0]] = part
                continue
            own_part = sums[len(columns)]
            keep = jnp.where(swap, part, own_part)
            given.append(jnp.where(swap, own_part, part).astype(jnp.bfloat16))
            back.append(exchange(behind(given[-1], back[-1] if back else None), "snap", cut))
            columns.append(keep + back[-1].astype(jnp.float32))

    for piece, low, bit in hops_in_order(OWN_WIDTHS + MATE_WIDTHS, cut):
        earlier = sent.setdefault(bit, [])
        depth = 2 if bit == 1 else 1
        ties = earlier[-depth] if len(earlier) >= depth else None
        held[piece][low | bit] = exchange(behind(held[piece][low], ties), "snap", bit)
        earlier.append(held[piece][low | bit])
        while len(halves) < len(BATCHES) and all(
            len(held[n]) == cut for numbers in BATCHES[len(halves)] for n in numbers
        ):
            add_batch()
    return jnp.concatenate(columns, axis=2)[:, None]


def solution(mesh):
    in_specs = (P("space", "snap"), P("space"), P())
    out_specs = P(None, "snap", "space", None)
    return jax.shard_map(body, mesh=mesh, in_specs=in_specs, out_specs=out_specs, check_vma=False)
```

```python
import jax
import jax.numpy as jnp
from jax import lax
from jax.experimental import pallas as pl
from jax.experimental.pallas import tpu as pltpu
from jax.sharding import PartitionSpec as P

ROUNDS = 4
OWN_WIDTHS = (2, 2)
MATE_WIDTHS = (2, 1, 1)
NEAR_FIRST = (3,)
VMEM = pl.BlockSpec(memory_space=pltpu.VMEM)
PARAMS = pltpu.CompilerParams(vmem_limit_bytes=40 * 2**20)


def exchange(part, axis, mask):
    return lax.ppermute(part, axis, [(i, i ^ mask) for i in range(lax.axis_size(axis))])


def behind(value, earlier):
    return value if earlier is None else lax.optimization_barrier((value, earlier))[0]


def hops_in_order(widths, cut):
    waiting = []
    for piece in range(len(widths)):
        bits, held = [1 << n for n in range(cut.bit_length() - 1)], [0]
        for bit in bits if piece in NEAR_FIRST else reversed(bits):
            waiting += [(piece, low, bit) for low in held]
            held += [low | bit for low in held]
    ready, crossed = {}, 0
    for piece, width in enumerate(widths):
        crossed += 2 * width if piece >= len(OWN_WIDTHS) else 0
        ready[piece, 0] = crossed
    free, ordered = {}, []
    while waiting:
        def start_of(hop):
            return max(free.get(hop[2], 0), ready[hop[:2]])

        able = [hop for hop in waiting if hop[:2] in ready]
        hop = min(able, key=lambda one: (start_of(one), waiting.index(one)))
        piece, low, bit = hop
        shared = 2 if bit == cut // 2 and start_of(hop) < crossed else 1
        free[bit] = ready[piece, low | bit] = start_of(hop) + shared * widths[piece]
        waiting.remove(hop)
        ordered.append(hop)
    return ordered


def gathered(pieces, widths, cut):
    held = [{0: piece} for piece in pieces]
    behind_of = {}
    for piece, low, bit in hops_in_order(widths, cut):
        earlier = behind_of.setdefault(bit, [])
        depth = 2 if bit == 1 else 1
        block = behind(held[piece][low], earlier[-depth] if len(earlier) >= depth else None)
        held[piece][low | bit] = exchange(block, "snap", bit)
        earlier.append(held[piece][low | bit])
    return [[found[low] for low in range(cut)] for found in held]


def turned(own, mate):
    cells = own[0].shape[0]
    group = sum(piece.shape[1] for piece in own)

    def kernel(*refs):
        out_ref = refs[-1]
        for which, some in enumerate((refs[: len(own)], refs[len(own) : -1])):
            first = 0
            for ref in some:
                out_ref[which, first : first + ref.shape[1], :] = ref[...].T
                first += ref.shape[1]

    return pl.pallas_call(
        kernel,
        out_shape=jax.ShapeDtypeStruct((2, group, cells), own[0].dtype),
        in_specs=[VMEM] * (len(own) + len(mate)),
        out_specs=VMEM,
        compiler_params=PARAMS,
        cost_estimate=pl.CostEstimate(
            flops=0, bytes_accessed=8 * group * cells, transcendentals=0
        ),
    )(*own, *mate)


def products(choices, lefts, blocks, scale_factor):
    slab_count = lax.axis_size("space")
    group, cells = lefts.shape[1:]
    width = blocks[0].shape[1]
    rows = group // slab_count

    def kernel(choices_ref, lefts_ref, *refs):
        block_refs = refs[: len(blocks)]
        out_ref, picked = refs[len(blocks) :]

        def one_round(round_number, carry):
            for number, block_ref in enumerate(block_refs):

                @pl.when(choices_ref[round_number] == number)
                def _():
                    picked[...] = block_ref[...]

            left = lefts_ref[choices_ref[ROUNDS + round_number]]
            tile = scale_factor * jnp.dot(left, picked[...], preferred_element_type=jnp.float32)
            for number in range(slab_count):
                part = tile[number * rows : (number + 1) * rows, :]
                out_ref[number, round_number] = part.astype(out_ref.dtype)
            return carry

        lax.fori_loop(0, ROUNDS, one_round, 0)

    return pl.pallas_call(
        kernel,
        out_shape=jax.ShapeDtypeStruct((slab_count, ROUNDS, rows, width), jnp.bfloat16),
        in_specs=[pl.BlockSpec(memory_space=pltpu.SMEM)] + [VMEM] * (1 + len(blocks)),
        out_specs=VMEM,
        scratch_shapes=[pltpu.VMEM((cells, width), jnp.bfloat16)],
        compiler_params=PARAMS,
        cost_estimate=pl.CostEstimate(
            flops=2 * ROUNDS * group * cells * width,
            bytes_accessed=2 * (lefts.size + (len(blocks) * cells + ROUNDS * group) * width),
            transcendentals=0,
        ),
    )(choices, lefts, *blocks)


def summed(parts):
    arrived = lax.all_to_all(parts, "space", 0, 0)
    return jnp.sum(arrived.astype(jnp.float32), axis=0)


def body(snapshots, volume, masks):
    slab_count = lax.axis_size("space")
    groups = lax.axis_size("snap")
    cut = groups // 2
    cells, group = snapshots.shape
    quarter = group // 4
    scale_factor = float(cells * slab_count) ** (-0.5)
    half = cells // 2
    place = lax.axis_index("snap").astype(jnp.int32)
    upper = (place >= cut).astype(jnp.int32)
    roots = jnp.sqrt(volume)[:, None]

    def pieces_of(side, widths):
        scale = lax.dynamic_slice_in_dim(roots, side * half, half)
        found, first = [], 0
        for width in widths:
            part = lax.dynamic_slice(
                snapshots, (side * half, first * quarter), (half, width * quarter)
            )
            found.append((part.astype(jnp.float32) * scale).astype(jnp.bfloat16))
            first += width
        return found

    mate, crossed = [], None
    for piece in pieces_of(1 - upper, MATE_WIDTHS):
        crossed = exchange(behind(piece, crossed), "snap", cut)
        mate.append(crossed)
    own = pieces_of(upper, OWN_WIDTHS)
    lefts = turned(own, mate)
    blocks = gathered(own + mate, OWN_WIDTHS + MATE_WIDTHS, cut)

    low = jnp.bitwise_and(masks, cut - 1)
    crossing = (masks >= cut).astype(jnp.int32)
    own_choices = jnp.concatenate([low, crossing])
    mate_choices = jnp.concatenate([low, 1 - crossing])

    own_sum = jnp.concatenate(
        [
            summed(products(own_choices, lefts, found, scale_factor))
            for found in blocks[: len(own)]
        ],
        axis=2,
    )
    swap = (crossing == 1)[:, None, None]
    columns, first = [], 0
    for found in blocks[len(own) :]:
        mate_sum = summed(products(mate_choices, lefts, found, scale_factor))
        held = lax.slice_in_dim(own_sum, first, first + mate_sum.shape[2], axis=2)
        keep = jnp.where(swap, mate_sum, held)
        give = jnp.where(swap, held, mate_sum).astype(jnp.bfloat16)
        columns.append(keep + exchange(give, "snap", cut).astype(jnp.float32))
        first += mate_sum.shape[2]
    return jnp.concatenate(columns, axis=2)[:, None]


def solution(mesh):
    in_specs = (P("space", "snap"), P("space"), P())
    out_specs = P(None, "snap", "space", None)
    return jax.shard_map(body, mesh=mesh, in_specs=in_specs, out_specs=out_specs, check_vma=False)
```

```python
import jax
import jax.numpy as jnp
from jax import lax
from jax.experimental import pallas as pl
from jax.experimental.pallas import tpu as pltpu
from jax.sharding import PartitionSpec as P

ROUNDS = 4
OWN_WIDTHS = (2, 2)
CROSSING_WIDTHS = (2, 2)
MATE_WIDTHS = (2, 1, 1)
NEAR_FIRST = (3,)
URGENCY = (0, 2, 1, 3, 4)
BATCHES = (((0,), (2,)), ((1,), (3, 4)))
VMEM = pl.BlockSpec(memory_space=pltpu.VMEM)
PARAMS = pltpu.CompilerParams(vmem_limit_bytes=40 * 2**20)


def exchange(part, axis, mask):
    return lax.ppermute(part, axis, [(i, i ^ mask) for i in range(lax.axis_size(axis))])


def behind(value, earlier):
    return value if earlier is None else lax.optimization_barrier((value, earlier))[0]


def hops_in_order(widths, cut):
    waiting = []
    for piece in URGENCY:
        bits, held = [1 << n for n in range(cut.bit_length() - 1)], [0]
        for bit in bits if piece in NEAR_FIRST else reversed(bits):
            waiting += [(piece, low, bit) for low in held]
            held += [low | bit for low in held]
    ready, crossed = {}, 0
    for piece, width in enumerate(widths):
        crossed += 2 * width if piece >= len(OWN_WIDTHS) else 0
        ready[piece, 0] = crossed
    free, ordered = {}, []
    while waiting:
        def start_of(hop):
            return max(free.get(hop[2], 0), ready[hop[:2]])

        able = [hop for hop in waiting if hop[:2] in ready]
        hop = min(able, key=lambda one: (start_of(one), -one[2], waiting.index(one)))
        piece, low, bit = hop
        shared = 2 if bit == cut // 2 and start_of(hop) < crossed else 1
        free[bit] = start_of(hop) + shared * widths[piece]
        ready[piece, low | bit] = free[bit]
        waiting.remove(hop)
        ordered.append(hop)
    return ordered


def turned(own, mate):
    cells = own[0].shape[0]
    group = sum(piece.shape[1] for piece in own)

    def kernel(*refs):
        out_ref = refs[-1]
        for which, some in enumerate((refs[: len(own)], refs[len(own) : -1])):
            first = 0
            for ref in some:
                out_ref[which, first : first + ref.shape[1], :] = ref[...].T
                first += ref.shape[1]

    return pl.pallas_call(
        kernel,
        out_shape=jax.ShapeDtypeStruct((2, group, cells), own[0].dtype),
        in_specs=[VMEM] * (len(own) + len(mate)),
        out_specs=VMEM,
        compiler_params=PARAMS,
        cost_estimate=pl.CostEstimate(flops=0, bytes_accessed=0, transcendentals=0),
    )(*own, *mate)


def products(choices, lefts, batch, scale_factor):
    slab_count = lax.axis_size("space")
    group, cells = lefts.shape[1:]
    widths = [sum(blocks[0].shape[1] for blocks in pieces) for _, pieces in batch]
    rows = group // slab_count
    arrays = [block for _, pieces in batch for blocks in pieces for block in blocks]

    def kernel(choices_ref, lefts_ref, *refs):
        waiting = list(refs[: len(arrays)])
        even_ref, odd_ref, picked, tile = refs[len(arrays) :]
        first = 0
        for (mates, pieces), width in zip(batch, widths):
            sources = [[waiting.pop(0) for _ in blocks] for blocks in pieces]
            columns = pl.ds(first, width)
            first += width

            def one_round(round_number, carry):
                begin = 0
                for block_refs in sources:
                    end = begin + block_refs[0].shape[1]
                    for number, block_ref in enumerate(block_refs):

                        @pl.when(choices_ref[round_number] == number)
                        def _():
                            picked[:, begin:end] = block_ref[...]

                    begin = end
                side = choices_ref[ROUNDS + round_number]
                left = lefts_ref[1 - side if mates else side]
                tile[:, :width] = scale_factor * jnp.dot(
                    left, picked[:, :width], preferred_element_type=jnp.float32
                )
                for number in range(slab_count):
                    start = jnp.bitwise_xor(choices_ref[2 * ROUNDS], number) * rows
                    part = tile[pl.ds(pl.multiple_of(start, rows), rows), :width]
                    out_ref = odd_ref if number % 2 else even_ref
                    out_ref[number // 2, round_number, :, columns] = part.astype(out_ref.dtype)
                return carry

            lax.fori_loop(0, ROUNDS, one_round, 0)

    shape = (slab_count // 2, ROUNDS, rows, sum(widths))
    return pl.pallas_call(
        kernel,
        out_shape=[jax.ShapeDtypeStruct(shape, kind) for kind in (jnp.float32, jnp.bfloat16)],
        in_specs=[pl.BlockSpec(memory_space=pltpu.SMEM)] + [VMEM] * (1 + len(arrays)),
        out_specs=[VMEM, VMEM],
        scratch_shapes=[
            pltpu.VMEM((cells, max(widths)), jnp.bfloat16),
            pltpu.VMEM((group, max(widths)), jnp.float32),
        ],
        compiler_params=PARAMS,
        cost_estimate=pl.CostEstimate(flops=0, bytes_accessed=0, transcendentals=0),
    )(choices, lefts, *arrays)


def halved(keep, send, bit):
    return keep + exchange(send, "space", bit).astype(jnp.float32)


def summed(total):
    bit = 2
    while len(total) > 1:
        total = halved(total[0::2], total[1::2].astype(jnp.bfloat16), bit)
        bit *= 2
    return total[0]


def body(snapshots, volume, masks):
    slab_count = lax.axis_size("space")
    groups = lax.axis_size("snap")
    cut = groups // 2
    cells, group = snapshots.shape
    quarter = group // 4
    scale_factor = float(cells * slab_count) ** (-0.5)
    half = cells // 2
    place = lax.axis_index("snap").astype(jnp.int32)
    upper = (place >= cut).astype(jnp.int32)
    roots = jnp.sqrt(volume)[:, None]

    def pieces_of(side, widths):
        scale = lax.dynamic_slice_in_dim(roots, side * half, half)
        found, first = [], 0
        for width in widths:
            part = lax.dynamic_slice(
                snapshots, (side * half, first * quarter), (half, width * quarter)
            )
            found.append((part.astype(jnp.float32) * scale).astype(jnp.bfloat16))
            first += width
        return found

    crossed = []
    for piece in pieces_of(1 - upper, CROSSING_WIDTHS):
        crossed.append(exchange(behind(piece, crossed[-1] if crossed else None), "snap", cut))
    own = pieces_of(upper, OWN_WIDTHS)
    lefts = turned(own, crossed)
    mate = []
    for width in MATE_WIDTHS:
        first = sum(piece.shape[1] for piece in mate)
        for piece in crossed:
            if first < piece.shape[1]:
                break
            first -= piece.shape[1]
        mate.append(lax.slice_in_dim(piece, first, first + width * quarter, axis=1))

    low = jnp.bitwise_and(masks, cut - 1)
    crossing = (masks >= cut).astype(jnp.int32)
    me = lax.axis_index("space").astype(jnp.int32)[None]
    choices = jnp.concatenate([low, crossing, me])
    swap = (crossing == 1)[:, None, None]

    held = [{0: piece} for piece in own + mate]
    sent = {}
    halves, given, sums, columns, back = [], [], {}, [], []

    def add_batch():
        lists = BATCHES[len(halves)]
        batch = [
            (numbers[0] >= len(own), [[held[n][low] for low in range(cut)] for n in numbers])
            for numbers in lists
        ]
        earlier = None
        if not halves:
            earlier = sent[cut // 2][-1]
        if lists == BATCHES[-1]:
            earlier = (given[0], halves[-1])
        even, odd = products(behind(choices, earlier), lefts, batch, scale_factor)
        halves.append(halved(even, odd, 1))
        total = summed(halves[-1])
        taken = 0
        for (mates, pieces), numbers in zip(batch, lists):
            width = sum(found[0].shape[1] for found in pieces)
            part = lax.slice_in_dim(total, taken, taken + width, axis=2)
            taken += width
            if not mates:
                sums[numbers[0]] = part
                continue
            own_part = sums[len(columns)]
            keep = jnp.where(swap, part, own_part)
            given.append(jnp.where(swap, own_part, part).astype(jnp.bfloat16))
            back.append(exchange(behind(given[-1], back[-1] if back else None), "snap", cut))
            columns.append(keep + back[-1].astype(jnp.float32))

    for piece, low, bit in hops_in_order(OWN_WIDTHS + MATE_WIDTHS, cut):
        earlier = sent.setdefault(bit, [])
        depth = 2 if bit == 1 else 1
        ties = earlier[-depth] if len(earlier) >= depth else None
        if bit == 1 and low == 0 and halves and piece in BATCHES[-1][-1]:
            ties = (ties, halves[0])
        held[piece][low | bit] = exchange(behind(held[piece][low], ties), "snap", bit)
        earlier.append(held[piece][low | bit])
        while len(halves) < len(BATCHES) and all(
            len(held[n]) == cut for numbers in BATCHES[len(halves)] for n in numbers
        ):
            add_batch()
    return jnp.concatenate(columns, axis=2)[:, None]


def solution(mesh):
    in_specs = (P("space", "snap"), P("space"), P())
    out_specs = P(None, "snap", "space", None)
    return jax.shard_map(body, mesh=mesh, in_specs=in_specs, out_specs=out_specs, check_vma=False)
```

```python
import jax
import jax.numpy as jnp
from jax import lax
from jax.experimental import pallas as pl
from jax.experimental.pallas import tpu as pltpu
from jax.sharding import PartitionSpec as P

ROUNDS = 4
OWN_WIDTHS = (2, 2)
CROSSING_WIDTHS = (2, 2)
MATE_WIDTHS = (2, 1, 1)
NEAR_FIRST = (3,)
URGENCY = (0, 2, 1, 3, 4)
BATCHES = (((0,), (2,)), ((1,), (3, 4)))
VMEM = pl.BlockSpec(memory_space=pltpu.VMEM)
PARAMS = pltpu.CompilerParams(vmem_limit_bytes=40 * 2**20)


def exchange(part, axis, mask):
    return lax.ppermute(part, axis, [(i, i ^ mask) for i in range(lax.axis_size(axis))])


def behind(value, earlier):
    return value if earlier is None else lax.optimization_barrier((value, earlier))[0]


def hops_in_order(widths, cut):
    waiting = []
    for piece in URGENCY:
        bits, held = [1 << n for n in range(cut.bit_length() - 1)], [0]
        for bit in bits if piece in NEAR_FIRST else reversed(bits):
            waiting += [(piece, low, bit) for low in held]
            held += [low | bit for low in held]
    ready, crossed = {}, 0
    for piece, width in enumerate(widths):
        crossed += 2 * width if piece >= len(OWN_WIDTHS) else 0
        ready[piece, 0] = crossed
    free, ordered = {}, []
    while waiting:
        def start_of(hop):
            return max(free.get(hop[2], 0), ready[hop[:2]])

        able = [hop for hop in waiting if hop[:2] in ready]
        hop = min(able, key=lambda one: (start_of(one), -one[2], waiting.index(one)))
        piece, low, bit = hop
        shared = 2 if bit == cut // 2 and start_of(hop) < crossed else 1
        free[bit] = start_of(hop) + shared * widths[piece]
        ready[piece, low | bit] = free[bit]
        waiting.remove(hop)
        ordered.append(hop)
    return ordered


def turned(own, mate):
    cells = own[0].shape[0]
    group = sum(piece.shape[1] for piece in own)

    def kernel(*refs):
        out_ref = refs[-1]
        for which, some in enumerate((refs[: len(own)], refs[len(own) : -1])):
            first = 0
            for ref in some:
                out_ref[which, first : first + ref.shape[1], :] = ref[...].T
                first += ref.shape[1]

    return pl.pallas_call(
        kernel,
        out_shape=jax.ShapeDtypeStruct((2, group, cells), own[0].dtype),
        in_specs=[VMEM] * (len(own) + len(mate)),
        out_specs=VMEM,
        compiler_params=PARAMS,
        cost_estimate=pl.CostEstimate(flops=0, bytes_accessed=0, transcendentals=0),
    )(*own, *mate)


def products(choices, lefts, batch, scale_factor):
    slab_count = lax.axis_size("space")
    group, cells = lefts.shape[1:]
    widths = [sum(blocks[0].shape[1] for blocks in pieces) for _, pieces in batch]
    rows = group // slab_count
    arrays = [block for _, pieces in batch for blocks in pieces for block in blocks]

    def kernel(choices_ref, lefts_ref, *refs):
        waiting = list(refs[: len(arrays)])
        even_ref, odd_ref, tiles = refs[len(arrays) :]
        first = 0
        for (mates, pieces), width in zip(batch, widths):
            sources = [[waiting.pop(0) for _ in blocks] for blocks in pieces]
            columns = pl.ds(first, width)
            first += width

            for round_number in range(ROUNDS):
                parts = []
                for block_refs in sources:
                    part = block_refs[0][...]
                    for number, block_ref in enumerate(block_refs[1:], 1):
                        wanted = choices_ref[round_number] == number
                        part = jnp.where(wanted, block_ref[...], part)
                    parts.append(part)
                right = jnp.concatenate(parts, axis=1) if len(parts) > 1 else parts[0]
                side = choices_ref[ROUNDS + round_number]
                left = lefts_ref[1 - side if mates else side]
                tile = tiles.at[round_number % 2]
                tile[:, :width] = scale_factor * jnp.dot(
                    left, right, preferred_element_type=jnp.float32
                )
                for number in range(slab_count):
                    start = jnp.bitwise_xor(choices_ref[2 * ROUNDS], number) * rows
                    part = tile[pl.ds(pl.multiple_of(start, rows), rows), :width]
                    out_ref = odd_ref if number % 2 else even_ref
                    out_ref[number // 2, round_number, :, columns] = part.astype(out_ref.dtype)

    shape = (slab_count // 2, ROUNDS, rows, sum(widths))
    return pl.pallas_call(
        kernel,
        out_shape=[jax.ShapeDtypeStruct(shape, kind) for kind in (jnp.float32, jnp.bfloat16)],
        in_specs=[pl.BlockSpec(memory_space=pltpu.SMEM)] + [VMEM] * (1 + len(arrays)),
        out_specs=[VMEM, VMEM],
        scratch_shapes=[pltpu.VMEM((2, group, max(widths)), jnp.float32)],
        compiler_params=PARAMS,
        cost_estimate=pl.CostEstimate(flops=0, bytes_accessed=0, transcendentals=0),
    )(choices, lefts, *arrays)


def halved(keep, send, bit):
    return keep + exchange(send, "space", bit).astype(jnp.float32)


def summed(total):
    bit = 2
    while len(total) > 1:
        total = halved(total[0::2], total[1::2].astype(jnp.bfloat16), bit)
        bit *= 2
    return total[0]


def body(snapshots, volume, masks):
    slab_count = lax.axis_size("space")
    groups = lax.axis_size("snap")
    cut = groups // 2
    cells, group = snapshots.shape
    quarter = group // 4
    scale_factor = float(cells * slab_count) ** (-0.5)
    half = cells // 2
    place = lax.axis_index("snap").astype(jnp.int32)
    upper = (place >= cut).astype(jnp.int32)
    roots = jnp.sqrt(volume)[:, None]

    def pieces_of(side, widths):
        scale = lax.dynamic_slice_in_dim(roots, side * half, half)
        found, first = [], 0
        for width in widths:
            part = lax.dynamic_slice(
                behind(snapshots, found[0] if found else None),
                (side * half, first * quarter),
                (half, width * quarter),
            )
            found.append((part.astype(jnp.float32) * scale).astype(jnp.bfloat16))
            first += width
        return found

    crossed = []
    for piece in pieces_of(1 - upper, CROSSING_WIDTHS):
        crossed.append(exchange(behind(piece, crossed[-1] if crossed else None), "snap", cut))
    own = pieces_of(upper, OWN_WIDTHS)
    lefts = turned(own, crossed)
    mate = []
    for width in MATE_WIDTHS:
        first = sum(piece.shape[1] for piece in mate)
        for piece in crossed:
            if first < piece.shape[1]:
                break
            first -= piece.shape[1]
        mate.append(lax.slice_in_dim(piece, first, first + width * quarter, axis=1))

    low = jnp.bitwise_and(masks, cut - 1)
    crossing = (masks >= cut).astype(jnp.int32)
    me = lax.axis_index("space").astype(jnp.int32)[None]
    choices = jnp.concatenate([low, crossing, me])
    swap = (crossing == 1)[:, None, None]

    held = [{0: piece} for piece in own + mate]
    sent = {}
    halves, given, sums, columns, back = [], [], {}, [], []

    def add_batch():
        lists = BATCHES[len(halves)]
        batch = [
            (numbers[0] >= len(own), [[held[n][low] for low in range(cut)] for n in numbers])
            for numbers in lists
        ]
        earlier = None
        if not halves:
            earlier = sent[cut // 2][-1]
        if lists == BATCHES[-1]:
            earlier = (given[0], halves[-1])
        even, odd = products(behind(choices, earlier), lefts, batch, scale_factor)
        halves.append(halved(even, odd, 1))
        total = summed(halves[-1])
        taken = 0
        for (mates, pieces), numbers in zip(batch, lists):
            width = sum(found[0].shape[1] for found in pieces)
            part = lax.slice_in_dim(total, taken, taken + width, axis=2)
            taken += width
            if not mates:
                sums[numbers[0]] = part
                continue
            own_part = sums[len(columns)]
            keep = jnp.where(swap, part, own_part)
            given.append(jnp.where(swap, own_part, part).astype(jnp.bfloat16))
            back.append(exchange(behind(given[-1], back[-1] if back else None), "snap", cut))
            columns.append(keep + back[-1].astype(jnp.float32))

    for piece, low, bit in hops_in_order(OWN_WIDTHS + MATE_WIDTHS, cut):
        earlier = sent.setdefault(bit, [])
        depth = 2 if bit == 1 else 1
        ties = earlier[-depth] if len(earlier) >= depth else None
        if bit == 1 and low == 0 and halves and piece in BATCHES[-1][-1]:
            ties = (ties, halves[0])
        held[piece][low | bit] = exchange(behind(held[piece][low], ties), "snap", bit)
        earlier.append(held[piece][low | bit])
        while len(halves) < len(BATCHES) and all(
            len(held[n]) == cut for numbers in BATCHES[len(halves)] for n in numbers
        ):
            add_batch()
    return jnp.concatenate(columns, axis=2)[:, None]


def solution(mesh):
    in_specs = (P("space", "snap"), P("space"), P())
    out_specs = P(None, "snap", "space", None)
    return jax.shard_map(body, mesh=mesh, in_specs=in_specs, out_specs=out_specs, check_vma=False)
```

```python
import jax
import jax.numpy as jnp
from jax import lax
from jax.experimental import pallas as pl
from jax.experimental.pallas import tpu as pltpu
from jax.sharding import PartitionSpec as P

ROUNDS = 4
OWN_WIDTHS = (2, 2)
CROSSING_WIDTHS = (2, 2)
MATE_WIDTHS = (2, 1, 1)
NEAR_FIRST = (3,)
URGENCY = (0, 2, 1, 3, 4)
BATCHES = (((0,), (2,)), ((1,), (3, 4)))
VMEM = pl.BlockSpec(memory_space=pltpu.VMEM)
PARAMS = pltpu.CompilerParams(vmem_limit_bytes=40 * 2**20)


def exchange(part, axis, mask):
    return lax.ppermute(part, axis, [(i, i ^ mask) for i in range(lax.axis_size(axis))])


def behind(value, earlier):
    return value if earlier is None else lax.optimization_barrier((value, earlier))[0]


def hops_in_order(widths, cut):
    waiting = []
    for piece in URGENCY:
        bits, held = [1 << n for n in range(cut.bit_length() - 1)], [0]
        for bit in bits if piece in NEAR_FIRST else reversed(bits):
            waiting += [(piece, low, bit) for low in held]
            held += [low | bit for low in held]
    ready, crossed = {}, 0
    for piece, width in enumerate(widths):
        crossed += 2 * width if piece >= len(OWN_WIDTHS) else 0
        ready[piece, 0] = crossed
    free, ordered = {}, []
    while waiting:
        def start_of(hop):
            return max(free.get(hop[2], 0), ready[hop[:2]])

        able = [hop for hop in waiting if hop[:2] in ready]
        hop = min(able, key=lambda one: (start_of(one), -one[2], waiting.index(one)))
        piece, low, bit = hop
        shared = 2 if bit == cut // 2 and start_of(hop) < crossed else 1
        free[bit] = start_of(hop) + shared * widths[piece]
        ready[piece, low | bit] = free[bit]
        waiting.remove(hop)
        ordered.append(hop)
    return ordered


def turned(own, mate):
    cells = own[0].shape[0]
    group = sum(piece.shape[1] for piece in own)

    def kernel(*refs):
        out_ref = refs[-1]
        for which, some in enumerate((refs[: len(own)], refs[len(own) : -1])):
            first = 0
            for ref in some:
                out_ref[which, first : first + ref.shape[1], :] = ref[...].T
                first += ref.shape[1]

    return pl.pallas_call(
        kernel,
        out_shape=jax.ShapeDtypeStruct((2, group, cells), own[0].dtype),
        in_specs=[VMEM] * (len(own) + len(mate)),
        out_specs=VMEM,
        compiler_params=PARAMS,
        cost_estimate=pl.CostEstimate(flops=0, bytes_accessed=0, transcendentals=0),
    )(*own, *mate)


def products(choices, lefts, batch, scale_factor):
    slab_count = lax.axis_size("space")
    group, cells = lefts.shape[1:]
    width = sum(blocks[0].shape[1] for blocks in batch[0])
    rows = group // slab_count
    arrays = [block for pieces in batch for blocks in pieces for block in blocks]

    def kernel(choices_ref, lefts_ref, *refs):
        waiting = list(refs[: len(arrays)])
        even_ref, odd_ref, tiles = refs[len(arrays) :]
        for mates, pieces in enumerate(batch):
            sources = [[waiting.pop(0) for _ in blocks] for blocks in pieces]
            for round_number in range(ROUNDS):
                parts = []
                for block_refs in sources:
                    part = block_refs[0][...]
                    for number, block_ref in enumerate(block_refs[1:], 1):
                        wanted = choices_ref[round_number] == number
                        part = jnp.where(wanted, block_ref[...], part)
                    parts.append(part)
                right = jnp.concatenate(parts, axis=1) if len(parts) > 1 else parts[0]
                side = choices_ref[ROUNDS + round_number]
                side = 1 - side if mates else side
                tile = tiles.at[round_number % 2]
                tile[...] = scale_factor * jnp.dot(
                    lefts_ref[side], right, preferred_element_type=jnp.float32
                )
                for number in range(slab_count):
                    start = jnp.bitwise_xor(choices_ref[2 * ROUNDS], number) * rows
                    part = tile[pl.ds(pl.multiple_of(start, rows), rows), :]
                    out_ref = odd_ref if number % 2 else even_ref
                    out_ref[side, number // 2, round_number] = part.astype(out_ref.dtype)

    shape = (2, slab_count // 2, ROUNDS, rows, width)
    return pl.pallas_call(
        kernel,
        out_shape=[jax.ShapeDtypeStruct(shape, kind) for kind in (jnp.float32, jnp.bfloat16)],
        in_specs=[pl.BlockSpec(memory_space=pltpu.SMEM)] + [VMEM] * (1 + len(arrays)),
        out_specs=[VMEM, VMEM],
        scratch_shapes=[pltpu.VMEM((2, group, width), jnp.float32)],
        compiler_params=PARAMS,
        cost_estimate=pl.CostEstimate(flops=0, bytes_accessed=0, transcendentals=0),
    )(choices, lefts, *arrays)


def halved(keep, send, bit):
    return keep + exchange(send, "space", bit).astype(jnp.float32)


def summed(total, earlier):
    bit = 2
    while len(total) > 1:
        send = behind(total[1::2].astype(jnp.bfloat16), earlier)
        total = halved(total[0::2], send, bit)
        bit *= 2
    return total[0]


def body(snapshots, volume, masks):
    slab_count = lax.axis_size("space")
    groups = lax.axis_size("snap")
    cut = groups // 2
    cells, group = snapshots.shape
    quarter = group // 4
    scale_factor = float(cells * slab_count) ** (-0.5)
    half = cells // 2
    place = lax.axis_index("snap").astype(jnp.int32)
    upper = (place >= cut).astype(jnp.int32)
    roots = jnp.sqrt(volume)[:, None]

    def pieces_of(side, widths):
        scale = lax.dynamic_slice_in_dim(roots, side * half, half)
        found, first = [], 0
        for width in widths:
            part = lax.dynamic_slice(
                behind(snapshots, found[0] if found else None),
                (side * half, first * quarter),
                (half, width * quarter),
            )
            found.append((part.astype(jnp.float32) * scale).astype(jnp.bfloat16))
            first += width
        return found

    crossed = []
    for piece in pieces_of(1 - upper, CROSSING_WIDTHS):
        crossed.append(exchange(behind(piece, crossed[-1] if crossed else None), "snap", cut))
    own = pieces_of(upper, OWN_WIDTHS)
    lefts = turned(own, crossed)
    mate = []
    for width in MATE_WIDTHS:
        first = sum(piece.shape[1] for piece in mate)
        for piece in crossed:
            if first < piece.shape[1]:
                break
            first -= piece.shape[1]
        mate.append(lax.slice_in_dim(piece, first, first + width * quarter, axis=1))

    low = jnp.bitwise_and(masks, cut - 1)
    crossing = (masks >= cut).astype(jnp.int32)
    rounds = jnp.concatenate([low, crossing])
    me = lax.axis_index("space").astype(jnp.int32)[None]

    held = [{0: piece} for piece in own + mate]
    sent = {}
    halves, columns, back = [], [], []

    def add_batch(rounds):
        batch = [
            [[held[n][low] for low in range(cut)] for n in numbers]
            for numbers in BATCHES[len(halves)]
        ]
        earlier = (columns, back) if halves else [arrived[-1] for arrived in sent.values()]
        rounds = exchange(behind(rounds, earlier), "space", 1)
        even, odd = products(jnp.concatenate([rounds, me]), lefts, batch, scale_factor)
        total = even + exchange(odd, "space", 1).astype(jnp.float32)
        halves.append(total)
        give = summed(total[1], None)
        back.append(exchange(give.astype(jnp.bfloat16), "snap", cut))
        columns.append(summed(total[0], give))
        return rounds

    for piece, low, bit in hops_in_order(OWN_WIDTHS + MATE_WIDTHS, cut):
        earlier = sent.setdefault(bit, [])
        depth = 2 if bit == 1 else 1
        ties = earlier[-depth] if len(earlier) >= depth else None
        if bit == 1 and low == 0 and halves and piece in BATCHES[-1][1]:
            ties = (ties, halves[0])
        held[piece][low | bit] = exchange(behind(held[piece][low], ties), "snap", bit)
        earlier.append(held[piece][low | bit])
        while len(halves) < len(BATCHES) and all(
            len(held[n]) == cut for numbers in BATCHES[len(halves)] for n in numbers
        ):
            rounds = add_batch(rounds)
    results = [kept + got.astype(jnp.float32) for kept, got in zip(columns, back)]
    return jnp.concatenate(results, axis=2)[:, None]


def solution(mesh):
    in_specs = (P("space", "snap"), P("space"), P())
    out_specs = P(None, "snap", "space", None)
    return jax.shard_map(body, mesh=mesh, in_specs=in_specs, out_specs=out_specs, check_vma=False)
```

```python
import jax
import jax.numpy as jnp
from jax import lax
from jax.experimental import pallas as pl
from jax.experimental.pallas import tpu as pltpu
from jax.sharding import PartitionSpec as P

ROUNDS = 4
OWN_WIDTHS = (2, 2)
CROSSING_WIDTHS = (2, 2)
MATE_WIDTHS = (2, 1, 1)
NEAR_FIRST = (3,)
URGENCY = (0, 2, 1, 3, 4)
BATCHES = (((0,), (2,)), ((1,), (3, 4)))
VMEM = pl.BlockSpec(memory_space=pltpu.VMEM)
PARAMS = pltpu.CompilerParams(vmem_limit_bytes=40 * 2**20)


def exchange(part, axis, mask):
    return lax.ppermute(part, axis, [(i, i ^ mask) for i in range(lax.axis_size(axis))])


def behind(value, earlier):
    return value if earlier is None else lax.optimization_barrier((value, earlier))[0]


def hops_in_order(widths, cut):
    waiting = []
    for piece in URGENCY:
        bits, held = [1 << n for n in range(cut.bit_length() - 1)], [0]
        for bit in bits if piece in NEAR_FIRST else reversed(bits):
            waiting += [(piece, low, bit) for low in held]
            held += [low | bit for low in held]
    ready, crossed = {}, 0
    for piece, width in enumerate(widths):
        crossed += 2 * width if piece >= len(OWN_WIDTHS) else 0
        ready[piece, 0] = crossed
    free, ordered = {}, []
    while waiting:
        def start_of(hop):
            return max(free.get(hop[2], 0), ready[hop[:2]])

        able = [hop for hop in waiting if hop[:2] in ready]
        hop = min(able, key=lambda one: (start_of(one), -one[2], waiting.index(one)))
        piece, low, bit = hop
        shared = 2 if bit == cut // 2 and start_of(hop) < crossed else 1
        free[bit] = start_of(hop) + shared * widths[piece]
        ready[piece, low | bit] = free[bit]
        waiting.remove(hop)
        ordered.append(hop)
    return ordered


def turned(own, mate):
    cells = own[0].shape[0]
    group = sum(piece.shape[1] for piece in own)

    def kernel(*refs):
        out_ref = refs[-1]
        for which, some in enumerate((refs[: len(own)], refs[len(own) : -1])):
            first = 0
            for ref in some:
                out_ref[which, first : first + ref.shape[1], :] = ref[...].T
                first += ref.shape[1]

    return pl.pallas_call(
        kernel,
        out_shape=jax.ShapeDtypeStruct((2, group, cells), own[0].dtype),
        in_specs=[VMEM] * (len(own) + len(mate)),
        out_specs=VMEM,
        compiler_params=PARAMS,
        cost_estimate=pl.CostEstimate(flops=0, bytes_accessed=0, transcendentals=0),
    )(*own, *mate)


def products(choices, lefts, batch, scale_factor):
    slab_count = lax.axis_size("space")
    group, cells = lefts.shape[1:]
    width = sum(blocks[0].shape[1] for blocks in batch[0])
    rows = group // slab_count
    arrays = [block for pieces in batch for blocks in pieces for block in blocks]

    def kernel(choices_ref, lefts_ref, *refs):
        waiting = list(refs[: len(arrays)])
        even_ref, odd_ref, tiles = refs[len(arrays) :]
        for mates, pieces in enumerate(batch):
            sources = [[waiting.pop(0) for _ in blocks] for blocks in pieces]
            for round_number in range(ROUNDS):
                parts = []
                for block_refs in sources:
                    part = block_refs[0][...]
                    for number, block_ref in enumerate(block_refs[1:], 1):
                        wanted = choices_ref[round_number] == number
                        part = jnp.where(wanted, block_ref[...], part)
                    parts.append(part)
                right = jnp.concatenate(parts, axis=1) if len(parts) > 1 else parts[0]
                side = choices_ref[ROUNDS + round_number]
                side = 1 - side if mates else side
                tile = tiles.at[round_number % 2]
                tile[...] = scale_factor * jnp.dot(
                    lefts_ref[side], right, preferred_element_type=jnp.float32
                )
                for number in range(slab_count):
                    start = jnp.bitwise_xor(choices_ref[2 * ROUNDS], number) * rows
                    part = tile[pl.ds(pl.multiple_of(start, rows), rows), :]
                    out_ref = odd_ref if number % 2 else even_ref
                    out_ref[side, number // 2, round_number] = part.astype(out_ref.dtype)

    shape = (2, slab_count // 2, ROUNDS, rows, width)
    return pl.pallas_call(
        kernel,
        out_shape=[jax.ShapeDtypeStruct(shape, kind) for kind in (jnp.float32, jnp.bfloat16)],
        in_specs=[pl.BlockSpec(memory_space=pltpu.SMEM)] + [VMEM] * (1 + len(arrays)),
        out_specs=[VMEM, VMEM],
        scratch_shapes=[pltpu.VMEM((2, group, width), jnp.float32)],
        compiler_params=PARAMS,
        cost_estimate=pl.CostEstimate(flops=0, bytes_accessed=0, transcendentals=0),
    )(choices, lefts, *arrays)


def halved(keep, send, bit):
    return keep + exchange(send, "space", bit).astype(jnp.float32)


def summed(total, earlier):
    bit = 2
    while len(total) > 1:
        send = behind(total[1::2].astype(jnp.bfloat16), earlier)
        total = halved(total[0::2], send, bit)
        bit *= 2
    return total[0]


def body(snapshots, volume, masks):
    slab_count = lax.axis_size("space")
    groups = lax.axis_size("snap")
    cut = groups // 2
    cells, group = snapshots.shape
    quarter = group // 4
    scale_factor = float(cells * slab_count) ** (-0.5)
    half = cells // 2
    place = lax.axis_index("snap").astype(jnp.int32)
    upper = (place >= cut).astype(jnp.int32)
    roots = jnp.sqrt(volume)[:, None]

    def pieces_of(side, widths):
        scale = lax.dynamic_slice_in_dim(roots, side * half, half)
        found, first = [], 0
        for width in widths:
            part = lax.dynamic_slice(
                behind(snapshots, found[0] if found else None),
                (side * half, first * quarter),
                (half, width * quarter),
            )
            found.append((part.astype(jnp.float32) * scale).astype(jnp.bfloat16))
            first += width
        return found

    crossed = []
    for piece in pieces_of(1 - upper, CROSSING_WIDTHS):
        crossed.append(exchange(behind(piece, crossed[-1] if crossed else None), "snap", cut))
    own = pieces_of(upper, OWN_WIDTHS)
    lefts = turned(own, crossed)
    mate = []
    for width in MATE_WIDTHS:
        first = sum(piece.shape[1] for piece in mate)
        for piece in crossed:
            if first < piece.shape[1]:
                break
            first -= piece.shape[1]
        mate.append(lax.slice_in_dim(piece, first, first + width * quarter, axis=1))

    low = jnp.bitwise_and(masks, cut - 1)
    crossing = (masks >= cut).astype(jnp.int32)
    rounds = jnp.concatenate([low, crossing])
    me = lax.axis_index("space").astype(jnp.int32)[None]

    held = [{0: piece} for piece in own + mate]
    sent = {}
    halves, columns, back = [], [], []

    def add_batch(rounds):
        batch = [
            [[held[n][low] for low in range(cut)] for n in numbers]
            for numbers in BATCHES[len(halves)]
        ]
        earlier = columns if halves else sent[cut // 2][-1]
        rounds = behind(rounds, earlier)
        even, odd = products(jnp.concatenate([rounds, me]), lefts, batch, scale_factor)
        total = even + exchange(odd, "space", 1).astype(jnp.float32)
        halves.append(total)
        give = summed(total[1], None)
        back.append(exchange(give.astype(jnp.bfloat16), "snap", cut))
        columns.append(summed(total[0], give))
        return rounds

    for piece, low, bit in hops_in_order(OWN_WIDTHS + MATE_WIDTHS, cut):
        earlier = sent.setdefault(bit, [])
        depth = (2 if len(earlier) < 7 else 3) if bit == 1 else 1
        ties = earlier[-depth] if len(earlier) >= depth else None
        held[piece][low | bit] = exchange(behind(held[piece][low], ties), "snap", bit)
        earlier.append(held[piece][low | bit])
        while len(halves) < len(BATCHES) and all(
            len(held[n]) == cut for numbers in BATCHES[len(halves)] for n in numbers
        ):
            rounds = add_batch(rounds)
    results = [kept + got.astype(jnp.float32) for kept, got in zip(columns, back)]
    return jnp.concatenate(results, axis=2)[:, None]


def solution(mesh):
    in_specs = (P("space", "snap"), P("space"), P())
    out_specs = P(None, "snap", "space", None)
    return jax.shard_map(body, mesh=mesh, in_specs=in_specs, out_specs=out_specs, check_vma=False)
```

```python
import jax
import jax.numpy as jnp
from jax import lax
from jax.experimental import pallas as pl
from jax.experimental.pallas import tpu as pltpu
from jax.sharding import PartitionSpec as P

ROUNDS = 4
OWN_WIDTHS = (2, 2)
CROSSING_WIDTHS = (2, 2)
MATE_WIDTHS = (2, 2)
NEAR_FIRST = (3,)
URGENCY = (0, 2, 1, 3)
BATCHES = (((0,), (2,)), ((1,), (3,)))
VMEM = pl.BlockSpec(memory_space=pltpu.VMEM)
PARAMS = pltpu.CompilerParams(vmem_limit_bytes=40 * 2**20)


def exchange(part, axis, mask):
    return lax.ppermute(part, axis, [(i, i ^ mask) for i in range(lax.axis_size(axis))])


def behind(value, earlier):
    return value if earlier is None else lax.optimization_barrier((value, earlier))[0]


def hops_in_order(widths, cut):
    waiting = []
    for piece in URGENCY:
        bits, held = [1 << n for n in range(cut.bit_length() - 1)], [0]
        for bit in bits if piece in NEAR_FIRST else reversed(bits):
            waiting += [(piece, low, bit) for low in held]
            held += [low | bit for low in held]
    ready, crossed = {}, 0
    for piece, width in enumerate(widths):
        crossed += 2 * width if piece >= len(OWN_WIDTHS) else 0
        ready[piece, 0] = crossed
    free, ordered = {}, []
    while waiting:
        def start_of(hop):
            return max(free.get(hop[2], 0), ready[hop[:2]])

        able = [hop for hop in waiting if hop[:2] in ready]
        hop = min(able, key=lambda one: (start_of(one), -one[2], waiting.index(one)))
        piece, low, bit = hop
        shared = 2 if bit == cut // 2 and start_of(hop) < crossed else 1
        free[bit] = start_of(hop) + shared * widths[piece]
        ready[piece, low | bit] = free[bit] + 0.5
        waiting.remove(hop)
        ordered.append(hop)
    return ordered


def turned(own, mate):
    cells = own[0].shape[0]
    group = sum(piece.shape[1] for piece in own)

    def kernel(*refs):
        out_ref = refs[-1]
        for which, some in enumerate((refs[: len(own)], refs[len(own) : -1])):
            first = 0
            for ref in some:
                out_ref[which, first : first + ref.shape[1], :] = ref[...].T
                first += ref.shape[1]

    return pl.pallas_call(
        kernel,
        out_shape=jax.ShapeDtypeStruct((2, group, cells), own[0].dtype),
        in_specs=[VMEM] * (len(own) + len(mate)),
        out_specs=VMEM,
        compiler_params=PARAMS,
        cost_estimate=pl.CostEstimate(flops=0, bytes_accessed=0, transcendentals=0),
    )(*own, *mate)


def products(choices, lefts, batch, scale_factor):
    slab_count = lax.axis_size("space")
    group, cells = lefts.shape[1:]
    width = sum(blocks[0].shape[1] for blocks in batch[0])
    rows = group // slab_count
    arrays = [block for pieces in batch for blocks in pieces for block in blocks]

    def kernel(choices_ref, lefts_ref, *refs):
        waiting = list(refs[: len(arrays)])
        even_ref, odd_ref, tiles = refs[len(arrays) :]
        for mates, pieces in enumerate(batch):
            sources = [[waiting.pop(0) for _ in blocks] for blocks in pieces]
            for round_number in range(ROUNDS):
                parts = []
                for block_refs in sources:
                    part = block_refs[0][...]
                    for number, block_ref in enumerate(block_refs[1:], 1):
                        wanted = choices_ref[round_number] == number
                        part = jnp.where(wanted, block_ref[...], part)
                    parts.append(part)
                right = jnp.concatenate(parts, axis=1) if len(parts) > 1 else parts[0]
                side = choices_ref[ROUNDS + round_number]
                side = 1 - side if mates else side
                tile = tiles.at[round_number % 2]
                tile[...] = scale_factor * jnp.dot(
                    lefts_ref[side], right, preferred_element_type=jnp.float32
                )
                for number in range(slab_count):
                    start = jnp.bitwise_xor(choices_ref[2 * ROUNDS], number) * rows
                    part = tile[pl.ds(pl.multiple_of(start, rows), rows), :]
                    out_ref = odd_ref if number % 2 else even_ref
                    out_ref[side, number // 2, round_number] = part.astype(out_ref.dtype)

    shape = (2, slab_count // 2, ROUNDS, rows, width)
    return pl.pallas_call(
        kernel,
        out_shape=[jax.ShapeDtypeStruct(shape, kind) for kind in (jnp.float32, jnp.bfloat16)],
        in_specs=[pl.BlockSpec(memory_space=pltpu.SMEM)] + [VMEM] * (1 + len(arrays)),
        out_specs=[VMEM, VMEM],
        scratch_shapes=[pltpu.VMEM((2, group, width), jnp.float32)],
        compiler_params=PARAMS,
        cost_estimate=pl.CostEstimate(flops=0, bytes_accessed=0, transcendentals=0),
    )(choices, lefts, *arrays)


def halved(keep, send, bit):
    return keep + exchange(send, "space", bit).astype(jnp.float32)


def summed(total, earlier):
    bit = 2
    while len(total) > 1:
        send = behind(total[1::2].astype(jnp.bfloat16), earlier)
        total = halved(total[0::2], send, bit)
        bit *= 2
    return total[0]


def body(snapshots, volume, masks):
    slab_count = lax.axis_size("space")
    groups = lax.axis_size("snap")
    cut = groups // 2
    cells, group = snapshots.shape
    quarter = group // 4
    scale_factor = float(cells * slab_count) ** (-0.5)
    half = cells // 2
    place = lax.axis_index("snap").astype(jnp.int32)
    upper = (place >= cut).astype(jnp.int32)
    roots = jnp.sqrt(volume)[:, None]

    def pieces_of(side, widths):
        scale = lax.dynamic_slice_in_dim(roots, side * half, half)
        found, first = [], 0
        for width in widths:
            part = lax.dynamic_slice(
                behind(snapshots, found[0] if found else None),
                (side * half, first * quarter),
                (half, width * quarter),
            )
            found.append((part.astype(jnp.float32) * scale).astype(jnp.bfloat16))
            first += width
        return found

    crossed = []
    for piece in pieces_of(1 - upper, CROSSING_WIDTHS):
        crossed.append(exchange(behind(piece, crossed[-1] if crossed else None), "snap", cut))
    own = pieces_of(upper, OWN_WIDTHS)
    lefts = turned(own, crossed)
    mate = []
    for width in MATE_WIDTHS:
        first = sum(piece.shape[1] for piece in mate)
        for piece in crossed:
            if first < piece.shape[1]:
                break
            first -= piece.shape[1]
        mate.append(lax.slice_in_dim(piece, first, first + width * quarter, axis=1))

    low = jnp.bitwise_and(masks, cut - 1)
    crossing = (masks >= cut).astype(jnp.int32)
    rounds = jnp.concatenate([low, crossing])
    me = lax.axis_index("space").astype(jnp.int32)[None]

    held = [{0: piece} for piece in own + mate]
    sent = {}
    halves, columns, back = [], [], []

    def add_batch(rounds):
        batch = [
            [[held[n][low] for low in range(cut)] for n in numbers]
            for numbers in BATCHES[len(halves)]
        ]
        earlier = columns if halves else sent[cut // 2][:3][-1]
        rounds = behind(rounds, earlier)
        even, odd = products(jnp.concatenate([rounds, me]), lefts, batch, scale_factor)
        total = even + exchange(odd, "space", 1).astype(jnp.float32)
        halves.append(total)
        give = summed(total[1], None)
        back.append(exchange(give.astype(jnp.bfloat16), "snap", cut))
        columns.append(summed(total[0], give))
        return rounds

    for piece, low, bit in hops_in_order(OWN_WIDTHS + MATE_WIDTHS, cut):
        earlier = sent.setdefault(bit, [])
        depth = 2 if bit == 1 and len(earlier) < 99 else 1
        ties = earlier[-depth] if len(earlier) >= depth else None
        held[piece][low | bit] = exchange(behind(held[piece][low], ties), "snap", bit)
        earlier.append(held[piece][low | bit])
        while len(halves) < len(BATCHES) and all(
            len(held[n]) == cut for numbers in BATCHES[len(halves)] for n in numbers
        ):
            rounds = add_batch(rounds)
    results = [kept + got.astype(jnp.float32) for kept, got in zip(columns, back)]
    return jnp.concatenate(results, axis=2)[:, None]


def solution(mesh):
    in_specs = (P("space", "snap"), P("space"), P())
    out_specs = P(None, "snap", "space", None)
    return jax.shard_map(body, mesh=mesh, in_specs=in_specs, out_specs=out_specs, check_vma=False)
```

```python
import jax
import jax.numpy as jnp
from jax import lax
from jax.experimental import pallas as pl
from jax.experimental.pallas import tpu as pltpu
from jax.sharding import PartitionSpec as P

ROUNDS = 4
OWN_WIDTHS = (2, 2)
CROSSING_WIDTHS = (2, 2)
MATE_WIDTHS = (2, 2)
NEAR_FIRST = (3,)
URGENCY = (0, 2, 1, 3)
BATCHES = (((0,), (2,)), ((1,), (3,)))
VMEM = pl.BlockSpec(memory_space=pltpu.VMEM)
PARAMS = pltpu.CompilerParams(vmem_limit_bytes=40 * 2**20)


def exchange(part, axis, mask):
    return lax.ppermute(part, axis, [(i, i ^ mask) for i in range(lax.axis_size(axis))])


def behind(value, earlier):
    return value if earlier is None else lax.optimization_barrier((value, earlier))[0]


def hops_in_order(widths, cut):
    waiting = []
    for piece in URGENCY:
        bits, held = [1 << n for n in range(cut.bit_length() - 1)], [0]
        for bit in bits if piece in NEAR_FIRST else reversed(bits):
            waiting += [(piece, low, bit) for low in held]
            held += [low | bit for low in held]
    ready, crossed = {}, 0
    for piece, width in enumerate(widths):
        crossed += 2 * width if piece >= len(OWN_WIDTHS) else 0
        ready[piece, 0] = crossed
    free, ordered = {}, []
    while waiting:
        def start_of(hop):
            return max(free.get(hop[2], 0), ready[hop[:2]])

        able = [hop for hop in waiting if hop[:2] in ready]
        hop = min(able, key=lambda one: (start_of(one), -one[2], waiting.index(one)))
        piece, low, bit = hop
        shared = 2 if bit == cut // 2 and start_of(hop) < crossed else 1
        free[bit] = start_of(hop) + shared * widths[piece]
        ready[piece, low | bit] = free[bit] + 0.5
        waiting.remove(hop)
        ordered.append(hop)
    return ordered


def turned(own, mate):
    cells = own[0].shape[0]
    group = sum(piece.shape[1] for piece in own)

    def kernel(*refs):
        out_ref = refs[-1]
        for which, some in enumerate((refs[: len(own)], refs[len(own) : -1])):
            first = 0
            for ref in some:
                out_ref[which, first : first + ref.shape[1], :] = ref[...].T
                first += ref.shape[1]

    return pl.pallas_call(
        kernel,
        out_shape=jax.ShapeDtypeStruct((2, group, cells), own[0].dtype),
        in_specs=[VMEM] * (len(own) + len(mate)),
        out_specs=VMEM,
        compiler_params=PARAMS,
        cost_estimate=pl.CostEstimate(flops=0, bytes_accessed=0, transcendentals=0),
    )(*own, *mate)


def products(choices, lefts, batch, scale_factor, side):
    slab_count = lax.axis_size("space")
    group, cells = lefts.shape[1:]
    width = sum(blocks[0].shape[1] for blocks in batch[0])
    rows = group // slab_count
    arrays = [block for pieces in batch for blocks in pieces for block in blocks]

    def kernel(choices_ref, lefts_ref, *refs):
        waiting = list(refs[: len(arrays)])
        even_ref, odd_ref, tiles = refs[len(arrays) :]
        sources = [[[waiting.pop(0) for _ in blocks] for blocks in pieces] for pieces in batch]

        def picked(pieces, round_number):
            parts = []
            for block_refs in pieces:
                part = block_refs[0][...]
                for number, block_ref in enumerate(block_refs[1:], 1):
                    wanted = choices_ref[round_number] == number
                    part = jnp.where(wanted, block_ref[...], part)
                parts.append(part)
            return jnp.concatenate(parts, axis=1) if len(parts) > 1 else parts[0]

        for round_number in range(ROUNDS):
            of_own = choices_ref[ROUNDS + round_number] == side
            own, mate = (picked(pieces, round_number) for pieces in sources)
            right = jnp.where(of_own, own, mate)
            tile = tiles.at[round_number % 2]
            tile[...] = scale_factor * jnp.dot(
                lefts_ref[side], right, preferred_element_type=jnp.float32
            )
            for number in range(slab_count):
                start = jnp.bitwise_xor(choices_ref[2 * ROUNDS], number) * rows
                part = tile[pl.ds(pl.multiple_of(start, rows), rows), :]
                out_ref = odd_ref if number % 2 else even_ref
                out_ref[number // 2, round_number] = part.astype(out_ref.dtype)

    shape = (slab_count // 2, ROUNDS, rows, width)
    return pl.pallas_call(
        kernel,
        out_shape=[jax.ShapeDtypeStruct(shape, kind) for kind in (jnp.float32, jnp.bfloat16)],
        in_specs=[pl.BlockSpec(memory_space=pltpu.SMEM)] + [VMEM] * (1 + len(arrays)),
        out_specs=[VMEM, VMEM],
        scratch_shapes=[pltpu.VMEM((2, group, width), jnp.float32)],
        compiler_params=PARAMS,
        cost_estimate=pl.CostEstimate(flops=0, bytes_accessed=0, transcendentals=0),
    )(choices, lefts, *arrays)


def halved(keep, send, bit):
    return keep + exchange(send, "space", bit).astype(jnp.float32)


def summed(total, earlier):
    bit = 2
    while len(total) > 1:
        send = behind(total[1::2].astype(jnp.bfloat16), earlier)
        total = halved(total[0::2], send, bit)
        bit *= 2
    return total[0]


def body(snapshots, volume, masks):
    slab_count = lax.axis_size("space")
    groups = lax.axis_size("snap")
    cut = groups // 2
    cells, group = snapshots.shape
    quarter = group // 4
    scale_factor = float(cells * slab_count) ** (-0.5)
    half = cells // 2
    place = lax.axis_index("snap").astype(jnp.int32)
    upper = (place >= cut).astype(jnp.int32)
    roots = jnp.sqrt(volume)[:, None]

    def pieces_of(side, widths):
        scale = lax.dynamic_slice_in_dim(roots, side * half, half)
        found, first = [], 0
        for width in widths:
            part = lax.dynamic_slice(
                behind(snapshots, found[0] if found else None),
                (side * half, first * quarter),
                (half, width * quarter),
            )
            found.append((part.astype(jnp.float32) * scale).astype(jnp.bfloat16))
            first += width
        return found

    crossed = []
    for piece in pieces_of(1 - upper, CROSSING_WIDTHS):
        crossed.append(exchange(behind(piece, crossed[-1] if crossed else None), "snap", cut))
    own = pieces_of(upper, OWN_WIDTHS)
    lefts = turned(own, crossed)
    mate = []
    for width in MATE_WIDTHS:
        first = sum(piece.shape[1] for piece in mate)
        for piece in crossed:
            if first < piece.shape[1]:
                break
            first -= piece.shape[1]
        mate.append(lax.slice_in_dim(piece, first, first + width * quarter, axis=1))

    low = jnp.bitwise_and(masks, cut - 1)
    crossing = (masks >= cut).astype(jnp.int32)
    rounds = jnp.concatenate([low, crossing])
    me = lax.axis_index("space").astype(jnp.int32)[None]

    held = [{0: piece} for piece in own + mate]
    sent = {}
    halves, columns, back = [], [], []

    def add_batch():
        batch = [
            [[held[n][low] for low in range(cut)] for n in numbers]
            for numbers in BATCHES[len(halves)]
        ]
        earlier = columns if halves else sent[cut // 2][:3][-1]
        choices = jnp.concatenate([behind(rounds, earlier), me])
        even, odd = products(choices, lefts, batch, scale_factor, 1)
        halves.append(halved(even, odd, 1))
        give = summed(halves[-1], None)
        back.append(exchange(give.astype(jnp.bfloat16), "snap", cut))
        even, odd = products(behind(choices, odd), lefts, batch, scale_factor, 0)
        columns.append(summed(halved(even, odd, 1), give))

    for piece, low, bit in hops_in_order(OWN_WIDTHS + MATE_WIDTHS, cut):
        earlier = sent.setdefault(bit, [])
        depth = 2 if bit == 1 and len(earlier) < 99 else 1
        ties = earlier[-depth] if len(earlier) >= depth else None
        held[piece][low | bit] = exchange(behind(held[piece][low], ties), "snap", bit)
        earlier.append(held[piece][low | bit])
        while len(halves) < len(BATCHES) and all(
            len(held[n]) == cut for numbers in BATCHES[len(halves)] for n in numbers
        ):
            add_batch()
    results = [kept + got.astype(jnp.float32) for kept, got in zip(columns, back)]
    return jnp.concatenate(results, axis=2)[:, None]


def solution(mesh):
    in_specs = (P("space", "snap"), P("space"), P())
    out_specs = P(None, "snap", "space", None)
    return jax.shard_map(body, mesh=mesh, in_specs=in_specs, out_specs=out_specs, check_vma=False)
```

```python
import jax
import jax.numpy as jnp
from jax import lax
from jax.experimental import pallas as pl
from jax.experimental.pallas import tpu as pltpu
from jax.sharding import PartitionSpec as P

ROUNDS = 4
OWN_WIDTHS = (2, 2)
CROSSING_WIDTHS = (2, 2)
MATE_WIDTHS = (2, 2)
NEAR_FIRST = (3,)
URGENCY = (0, 2, 1, 3)
BATCHES = (((0,), (2,)), ((1,), (3,)))
VMEM = pl.BlockSpec(memory_space=pltpu.VMEM)
SPARE = 6 * 2**20


def exchange(part, axis, mask):
    return lax.ppermute(part, axis, [(i, i ^ mask) for i in range(lax.axis_size(axis))])


def behind(value, earlier):
    return value if earlier is None else lax.optimization_barrier((value, earlier))[0]


def hops_in_order(widths, cut):
    waiting = []
    for piece in URGENCY:
        bits, held = [1 << n for n in range(cut.bit_length() - 1)], [0]
        for bit in bits if piece in NEAR_FIRST else reversed(bits):
            waiting += [(piece, low, bit) for low in held]
            held += [low | bit for low in held]
    ready, crossed = {}, 0
    for piece, width in enumerate(widths):
        crossed += 2 * width if piece >= len(OWN_WIDTHS) else 0
        ready[piece, 0] = crossed
    free, ordered = {}, []
    while waiting:
        def start_of(hop):
            return max(free.get(hop[2], 0), ready[hop[:2]])

        able = [hop for hop in waiting if hop[:2] in ready]
        hop = min(able, key=lambda one: (start_of(one), -one[2], waiting.index(one)))
        piece, low, bit = hop
        shared = 2 if bit == cut // 2 and start_of(hop) < crossed else 1
        free[bit] = start_of(hop) + shared * widths[piece]
        ready[piece, low | bit] = free[bit] + 0.5
        waiting.remove(hop)
        ordered.append(hop)
    return ordered


def turned(own, mate):
    cells = own[0].shape[0]
    group = sum(piece.shape[1] for piece in own)

    def kernel(*refs):
        out_ref = refs[-1]
        for which, some in enumerate((refs[: len(own)], refs[len(own) : -1])):
            first = 0
            for ref in some:
                out_ref[which, first : first + ref.shape[1], :] = ref[...].T
                first += ref.shape[1]

    return pl.pallas_call(
        kernel,
        out_shape=jax.ShapeDtypeStruct((2, group, cells), own[0].dtype),
        in_specs=[VMEM] * (len(own) + len(mate)),
        out_specs=VMEM,
        compiler_params=pltpu.CompilerParams(vmem_limit_bytes=8 * group * cells + SPARE),
        cost_estimate=pl.CostEstimate(flops=0, bytes_accessed=0, transcendentals=0),
    )(*own, *mate)


def products(choices, lefts, batch, scale_factor, side):
    slab_count = lax.axis_size("space")
    group, cells = lefts.shape[1:]
    width = sum(blocks[0].shape[1] for blocks in batch[0])
    rows = group // slab_count
    arrays = [block for pieces in batch for blocks in pieces for block in blocks]

    def kernel(choices_ref, lefts_ref, *refs):
        waiting = list(refs[: len(arrays)])
        even_ref, odd_ref, tiles = refs[len(arrays) :]
        sources = [[[waiting.pop(0) for _ in blocks] for blocks in pieces] for pieces in batch]

        def picked(pieces, round_number):
            parts = []
            for block_refs in pieces:
                part = block_refs[0][...]
                for number, block_ref in enumerate(block_refs[1:], 1):
                    wanted = choices_ref[round_number] == number
                    part = jnp.where(wanted, block_ref[...], part)
                parts.append(part)
            return jnp.concatenate(parts, axis=1) if len(parts) > 1 else parts[0]

        for round_number in range(ROUNDS):
            of_own = choices_ref[ROUNDS + round_number] == side
            own, mate = (picked(pieces, round_number) for pieces in sources)
            right = jnp.where(of_own, own, mate)
            tile = tiles.at[round_number % 2]
            tile[...] = scale_factor * jnp.dot(
                lefts_ref[side], right, preferred_element_type=jnp.float32
            )
            for number in range(slab_count):
                start = jnp.bitwise_xor(choices_ref[2 * ROUNDS], number) * rows
                part = tile[pl.ds(pl.multiple_of(start, rows), rows), :]
                out_ref = odd_ref if number % 2 else even_ref
                out_ref[number // 2, round_number] = part.astype(out_ref.dtype)

    shape = (slab_count // 2, ROUNDS, rows, width)
    need = 2 * (lefts.size + sum(array.size for array in arrays)) + (8 + 3 * ROUNDS) * group * width
    return pl.pallas_call(
        kernel,
        out_shape=[jax.ShapeDtypeStruct(shape, kind) for kind in (jnp.float32, jnp.bfloat16)],
        in_specs=[pl.BlockSpec(memory_space=pltpu.SMEM)] + [VMEM] * (1 + len(arrays)),
        out_specs=[VMEM, VMEM],
        scratch_shapes=[pltpu.VMEM((2, group, width), jnp.float32)],
        compiler_params=pltpu.CompilerParams(vmem_limit_bytes=need + SPARE),
        cost_estimate=pl.CostEstimate(flops=0, bytes_accessed=0, transcendentals=0),
    )(choices, lefts, *arrays)


def halved(keep, send, bit):
    return keep + exchange(send, "space", bit).astype(jnp.float32)


def summed(total, earlier):
    bit = 2
    while len(total) > 1:
        send = behind(total[1::2].astype(jnp.bfloat16), earlier)
        total = halved(total[0::2], send, bit)
        bit *= 2
    return total[0]


def body(snapshots, volume, masks):
    slab_count = lax.axis_size("space")
    groups = lax.axis_size("snap")
    cut = groups // 2
    cells, group = snapshots.shape
    quarter = group // 4
    scale_factor = float(cells * slab_count) ** (-0.5)
    half = cells // 2
    place = lax.axis_index("snap").astype(jnp.int32)
    upper = (place >= cut).astype(jnp.int32)
    roots = jnp.sqrt(volume)[:, None]

    def pieces_of(side, widths):
        scale = lax.dynamic_slice_in_dim(roots, side * half, half)
        found, first = [], 0
        for width in widths:
            part = lax.dynamic_slice(
                behind(snapshots, found[0] if found else None),
                (side * half, first * quarter),
                (half, width * quarter),
            )
            found.append((part.astype(jnp.float32) * scale).astype(jnp.bfloat16))
            first += width
        return found

    crossed = []
    for piece in pieces_of(1 - upper, CROSSING_WIDTHS):
        crossed.append(exchange(behind(piece, crossed[-1] if crossed else None), "snap", cut))
    own = pieces_of(upper, OWN_WIDTHS)
    lefts = turned(own, crossed)
    mate = []
    for width in MATE_WIDTHS:
        first = sum(piece.shape[1] for piece in mate)
        for piece in crossed:
            if first < piece.shape[1]:
                break
            first -= piece.shape[1]
        mate.append(lax.slice_in_dim(piece, first, first + width * quarter, axis=1))

    low = jnp.bitwise_and(masks, cut - 1)
    crossing = (masks >= cut).astype(jnp.int32)
    rounds = jnp.concatenate([low, crossing])
    me = lax.axis_index("space").astype(jnp.int32)[None]

    held = [{0: piece} for piece in own + mate]
    sent = {}
    halves, columns, back = [], [], []

    def add_batch():
        batch = [
            [[held[n][low] for low in range(cut)] for n in numbers]
            for numbers in BATCHES[len(halves)]
        ]
        earlier = columns if halves else sent[cut // 2][:3][-1]
        choices = jnp.concatenate([behind(rounds, earlier), me])
        even, odd = products(choices, lefts, batch, scale_factor, 1)
        halves.append(halved(even, odd, 1))
        give = summed(halves[-1], None)
        back.append(exchange(give.astype(jnp.bfloat16), "snap", cut))
        even, odd = products(behind(choices, odd), lefts, batch, scale_factor, 0)
        columns.append(summed(halved(even, odd, 1), give))

    for piece, low, bit in hops_in_order(OWN_WIDTHS + MATE_WIDTHS, cut):
        earlier = sent.setdefault(bit, [])
        depth = 2 if bit == 1 and len(earlier) < 99 else 1
        ties = earlier[-depth] if len(earlier) >= depth else None
        held[piece][low | bit] = exchange(behind(held[piece][low], ties), "snap", bit)
        earlier.append(held[piece][low | bit])
        while len(halves) < len(BATCHES) and all(
            len(held[n]) == cut for numbers in BATCHES[len(halves)] for n in numbers
        ):
            add_batch()
    results = [kept + got.astype(jnp.float32) for kept, got in zip(columns, back)]
    return jnp.concatenate(results, axis=2)[:, None]


def solution(mesh):
    in_specs = (P("space", "snap"), P("space"), P())
    out_specs = P(None, "snap", "space", None)
    return jax.shard_map(body, mesh=mesh, in_specs=in_specs, out_specs=out_specs, check_vma=False)
```

```python
from functools import partial

import jax
import jax.numpy as jnp
from jax import lax
from jax.experimental import pallas as pl
from jax.experimental.pallas import tpu as pltpu
from jax.sharding import PartitionSpec as P

ROUNDS = 4
OWN_WIDTHS = (2, 2)
CROSSING_WIDTHS = (2, 2)
MATE_WIDTHS = (2, 2)
NEAR_FIRST = (3,)
URGENCY = (0, 2, 1, 3)
BATCHES = (((0,), (2,)), ((1,), (3,)))
VMEM = pl.BlockSpec(memory_space=pltpu.VMEM)
PARAMS = pltpu.CompilerParams(vmem_limit_bytes=40 * 2**20)


def exchange(part, axis, mask):
    return lax.ppermute(part, axis, [(i, i ^ mask) for i in range(lax.axis_size(axis))])


def behind(value, earlier):
    return value if earlier is None else lax.optimization_barrier((value, earlier))[0]


def hops_in_order(widths, cut):
    waiting = []
    for piece in URGENCY:
        bits, held = [1 << n for n in range(cut.bit_length() - 1)], [0]
        for bit in bits if piece in NEAR_FIRST else reversed(bits):
            waiting += [(piece, low, bit) for low in held]
            held += [low | bit for low in held]
    ready, crossed = {}, 0
    for piece, width in enumerate(widths):
        crossed += 2 * width if piece >= len(OWN_WIDTHS) else 0
        ready[piece, 0] = crossed
    free, ordered = {}, []
    while waiting:
        def start_of(hop):
            return max(free.get(hop[2], 0), ready[hop[:2]])

        able = [hop for hop in waiting if hop[:2] in ready]
        hop = min(able, key=lambda one: (start_of(one), -one[2], waiting.index(one)))
        piece, low, bit = hop
        shared = 2 if bit == cut // 2 and start_of(hop) < crossed else 1
        free[bit] = start_of(hop) + shared * widths[piece]
        ready[piece, low | bit] = free[bit] + 0.5
        waiting.remove(hop)
        ordered.append(hop)
    return ordered


def turned(own, mate):
    cells = own[0].shape[0]
    group = sum(piece.shape[1] for piece in own)

    def kernel(*refs):
        out_ref = refs[-1]
        for which, some in enumerate((refs[: len(own)], refs[len(own) : -1])):
            first = 0
            for ref in some:
                out_ref[which, first : first + ref.shape[1], :] = ref[...].T
                first += ref.shape[1]

    return pl.pallas_call(
        kernel,
        out_shape=jax.ShapeDtypeStruct((2, group, cells), own[0].dtype),
        in_specs=[VMEM] * (len(own) + len(mate)),
        out_specs=VMEM,
        compiler_params=PARAMS,
        cost_estimate=pl.CostEstimate(flops=0, bytes_accessed=0, transcendentals=0),
    )(*own, *mate)


def products(choices, lefts, batch, scale_factor, side):
    slab_count = lax.axis_size("space")
    group, cells = lefts.shape[1:]
    width = sum(blocks[0].shape[1] for blocks in batch[0])
    rows = group // slab_count
    arrays = [block for pieces in batch for blocks in pieces for block in blocks]

    def kernel(choices_ref, lefts_ref, *refs):
        waiting = list(refs[: len(arrays)])
        even_ref, odd_ref, tiles = refs[len(arrays) :]
        sources = [[[waiting.pop(0) for _ in blocks] for blocks in pieces] for pieces in batch]

        def picked(pieces, round_number):
            parts = []
            for block_refs in pieces:
                part = block_refs[0][...]
                for number, block_ref in enumerate(block_refs[1:], 1):
                    wanted = choices_ref[round_number] == number
                    part = jnp.where(wanted, block_ref[...], part)
                parts.append(part)
            return jnp.concatenate(parts, axis=1) if len(parts) > 1 else parts[0]

        for round_number in range(ROUNDS):
            of_own = choices_ref[ROUNDS + round_number] == side
            own, mate = (picked(pieces, round_number) for pieces in sources)
            right = jnp.where(of_own, own, mate)
            tile = tiles.at[round_number % 2]
            tile[...] = scale_factor * jnp.dot(
                lefts_ref[side], right, preferred_element_type=jnp.float32
            )
            for number in range(slab_count):
                start = jnp.bitwise_xor(choices_ref[2 * ROUNDS], number) * rows
                part = tile[pl.ds(pl.multiple_of(start, rows), rows), :]
                out_ref = odd_ref if number % 2 else even_ref
                out_ref[number // 2, round_number] = part.astype(out_ref.dtype)

    shape = (slab_count // 2, ROUNDS, rows, width)
    return pl.pallas_call(
        kernel,
        out_shape=[jax.ShapeDtypeStruct(shape, kind) for kind in (jnp.float32, jnp.bfloat16)],
        in_specs=[pl.BlockSpec(memory_space=pltpu.SMEM)] + [VMEM] * (1 + len(arrays)),
        out_specs=[VMEM, VMEM],
        scratch_shapes=[pltpu.VMEM((2, group, width), jnp.float32)],
        compiler_params=PARAMS,
        cost_estimate=pl.CostEstimate(flops=0, bytes_accessed=0, transcendentals=0),
    )(choices, lefts, *arrays)


def halved(keep, send, bit):
    return keep + exchange(send, "space", bit).astype(jnp.float32)


def summed(total, earlier):
    bit = 2
    while len(total) > 1:
        send = behind(total[1::2].astype(jnp.bfloat16), earlier)
        total = halved(total[0::2], send, bit)
        bit *= 2
    return total[0]


def body(snapshots, volume, masks):
    slab_count = lax.axis_size("space")
    groups = lax.axis_size("snap")
    cut = groups // 2
    cells, group = snapshots.shape
    quarter = group // 4
    scale_factor = float(cells * slab_count) ** (-0.5)
    half = cells // 2
    place = lax.axis_index("snap").astype(jnp.int32)
    upper = (place >= cut).astype(jnp.int32)
    roots = jnp.sqrt(volume)[:, None]

    def pieces_of(side, widths):
        scale = lax.dynamic_slice_in_dim(roots, side * half, half)
        found, first = [], 0
        for width in widths:
            part = lax.dynamic_slice(
                behind(snapshots, found[0] if found else None),
                (side * half, first * quarter),
                (half, width * quarter),
            )
            found.append((part.astype(jnp.float32) * scale).astype(jnp.bfloat16))
            first += width
        return found

    crossed = []
    for piece in pieces_of(1 - upper, CROSSING_WIDTHS):
        crossed.append(exchange(behind(piece, crossed[-1] if crossed else None), "snap", cut))
    own = pieces_of(upper, OWN_WIDTHS)
    lefts = turned(own, crossed)
    mate = []
    for width in MATE_WIDTHS:
        first = sum(piece.shape[1] for piece in mate)
        for piece in crossed:
            if first < piece.shape[1]:
                break
            first -= piece.shape[1]
        mate.append(lax.slice_in_dim(piece, first, first + width * quarter, axis=1))

    low = jnp.bitwise_and(masks, cut - 1)
    crossing = (masks >= cut).astype(jnp.int32)
    rounds = jnp.concatenate([low, crossing])
    me = lax.axis_index("space").astype(jnp.int32)[None]

    held = [{0: piece} for piece in own + mate]
    sent = {}
    halves, columns, back, keeps = [], [], [], []

    def add_batch():
        batch = [
            [[held[n][low] for low in range(cut)] for n in numbers]
            for numbers in BATCHES[len(halves)]
        ]
        if keeps:
            keeps.pop()(held[len(own) - 1][cut - 1])
        earlier = columns if halves else sent[cut // 2][:3][-1]
        choices = jnp.concatenate([behind(rounds, earlier), me])
        even, odd = products(choices, lefts, batch, scale_factor, 1)
        halves.append(halved(even, odd, 1))
        give = summed(halves[-1], None)
        back.append(exchange(give.astype(jnp.bfloat16), "snap", cut))

        def keep(first, then):
            even, odd = products(behind(choices, first), lefts, batch, scale_factor, 0)
            columns.append(summed(halved(even, odd, 1), (give, then)))

        keeps.append(partial(keep, odd))

    for piece, low, bit in hops_in_order(OWN_WIDTHS + MATE_WIDTHS, cut):
        earlier = sent.setdefault(bit, [])
        depth = 2 if bit == 1 and len(earlier) < 99 else 1
        ties = earlier[-depth] if len(earlier) >= depth else None
        held[piece][low | bit] = exchange(behind(held[piece][low], ties), "snap", bit)
        earlier.append(held[piece][low | bit])
        while len(halves) < len(BATCHES) and all(
            len(held[n]) == cut for numbers in BATCHES[len(halves)] for n in numbers
        ):
            add_batch()
    keeps.pop()(None)
    results = [kept + got.astype(jnp.float32) for kept, got in zip(columns, back)]
    return jnp.concatenate(results, axis=2)[:, None]


def solution(mesh):
    in_specs = (P("space", "snap"), P("space"), P())
    out_specs = P(None, "snap", "space", None)
    return jax.shard_map(body, mesh=mesh, in_specs=in_specs, out_specs=out_specs, check_vma=False)
```

```python
from functools import partial

import jax
import jax.numpy as jnp
from jax import lax
from jax.experimental import pallas as pl
from jax.experimental.pallas import tpu as pltpu
from jax.sharding import PartitionSpec as P

ROUNDS = 4
OWN_WIDTHS = (2, 2)
CROSSING_WIDTHS = (2, 2)
MATE_WIDTHS = (2, 2)
NEAR_FIRST = ()
URGENCY = (0, 2, 1, 3)
BATCHES = (((0,), (2,)), ((1,), (3,)))
VMEM = pl.BlockSpec(memory_space=pltpu.VMEM)
PARAMS = pltpu.CompilerParams(vmem_limit_bytes=40 * 2**20)


def exchange(part, axis, mask):
    return lax.ppermute(part, axis, [(i, i ^ mask) for i in range(lax.axis_size(axis))])


def behind(value, earlier):
    return value if earlier is None else lax.optimization_barrier((value, earlier))[0]


def hops_in_order(widths, cut):
    waiting = []
    for piece in URGENCY:
        bits, held = [1 << n for n in range(cut.bit_length() - 1)], [0]
        for bit in bits if piece in NEAR_FIRST else reversed(bits):
            waiting += [(piece, low, bit) for low in held]
            held += [low | bit for low in held]
    ready, crossed = {}, 0
    for piece, width in enumerate(widths):
        crossed += 2 * width if piece >= len(OWN_WIDTHS) else 0
        ready[piece, 0] = crossed
    free, ordered = {}, []
    while waiting:
        def start_of(hop):
            return max(free.get(hop[2], 0), ready[hop[:2]])

        able = [hop for hop in waiting if hop[:2] in ready]
        hop = min(able, key=lambda one: (start_of(one), -one[2], waiting.index(one)))
        piece, low, bit = hop
        shared = 2 if bit == cut // 2 and start_of(hop) < crossed else 1
        free[bit] = start_of(hop) + shared * widths[piece]
        ready[piece, low | bit] = free[bit] + 0.5
        waiting.remove(hop)
        ordered.append(hop)
    return ordered


def turned(own, mate):
    cells = own[0].shape[0]
    group = sum(piece.shape[1] for piece in own)

    def kernel(*refs):
        out_ref = refs[-1]
        for which, some in enumerate((refs[: len(own)], refs[len(own) : -1])):
            first = 0
            for ref in some:
                out_ref[which, first : first + ref.shape[1], :] = ref[...].T
                first += ref.shape[1]

    return pl.pallas_call(
        kernel,
        out_shape=jax.ShapeDtypeStruct((2, group, cells), own[0].dtype),
        in_specs=[VMEM] * (len(own) + len(mate)),
        out_specs=VMEM,
        compiler_params=PARAMS,
        cost_estimate=pl.CostEstimate(flops=0, bytes_accessed=0, transcendentals=0),
    )(*own, *mate)


def products(choices, lefts, batch, scale_factor, side):
    slab_count = lax.axis_size("space")
    group, cells = lefts.shape[1:]
    width = sum(blocks[0].shape[1] for blocks in batch[0])
    rows = group // slab_count
    arrays = [block for pieces in batch for blocks in pieces for block in blocks]

    def kernel(choices_ref, lefts_ref, *refs):
        waiting = list(refs[: len(arrays)])
        even_ref, odd_ref, tiles = refs[len(arrays) :]
        sources = [[[waiting.pop(0) for _ in blocks] for blocks in pieces] for pieces in batch]

        def picked(pieces, round_number):
            parts = []
            for block_refs in pieces:
                part = block_refs[0][...]
                for number, block_ref in enumerate(block_refs[1:], 1):
                    wanted = choices_ref[round_number] == number
                    part = jnp.where(wanted, block_ref[...], part)
                parts.append(part)
            return jnp.concatenate(parts, axis=1) if len(parts) > 1 else parts[0]

        for round_number in range(ROUNDS):
            of_own = choices_ref[ROUNDS + round_number] == side
            own, mate = (picked(pieces, round_number) for pieces in sources)
            right = jnp.where(of_own, own, mate)
            tile = tiles.at[round_number % 2]
            tile[...] = scale_factor * jnp.dot(
                lefts_ref[side], right, preferred_element_type=jnp.float32
            )
            for number in range(slab_count):
                start = jnp.bitwise_xor(choices_ref[2 * ROUNDS], number) * rows
                part = tile[pl.ds(pl.multiple_of(start, rows), rows), :]
                out_ref = odd_ref if number % 2 else even_ref
                out_ref[number // 2, round_number] = part.astype(out_ref.dtype)

    shape = (slab_count // 2, ROUNDS, rows, width)
    return pl.pallas_call(
        kernel,
        out_shape=[jax.ShapeDtypeStruct(shape, kind) for kind in (jnp.float32, jnp.bfloat16)],
        in_specs=[pl.BlockSpec(memory_space=pltpu.SMEM)] + [VMEM] * (1 + len(arrays)),
        out_specs=[VMEM, VMEM],
        scratch_shapes=[pltpu.VMEM((2, group, width), jnp.float32)],
        compiler_params=PARAMS,
        cost_estimate=pl.CostEstimate(flops=0, bytes_accessed=0, transcendentals=0),
    )(choices, lefts, *arrays)


def halved(keep, send, bit):
    return keep + exchange(send, "space", bit).astype(jnp.float32)


def summed(total, earlier):
    bit = 2
    while len(total) > 1:
        send = behind(total[1::2].astype(jnp.bfloat16), earlier)
        total = halved(total[0::2], send, bit)
        bit *= 2
    return total[0]


def body(snapshots, volume, masks):
    slab_count = lax.axis_size("space")
    groups = lax.axis_size("snap")
    cut = groups // 2
    cells, group = snapshots.shape
    quarter = group // 4
    scale_factor = float(cells * slab_count) ** (-0.5)
    half = cells // 2
    place = lax.axis_index("snap").astype(jnp.int32)
    upper = (place >= cut).astype(jnp.int32)
    roots = jnp.sqrt(volume)[:, None]

    def pieces_of(side, widths):
        scale = lax.dynamic_slice_in_dim(roots, side * half, half)
        found, first = [], 0
        for width in widths:
            part = lax.dynamic_slice(
                behind(snapshots, found[0] if found else None),
                (side * half, first * quarter),
                (half, width * quarter),
            )
            found.append((part.astype(jnp.float32) * scale).astype(jnp.bfloat16))
            first += width
        return found

    crossed = []
    for piece in pieces_of(1 - upper, CROSSING_WIDTHS):
        crossed.append(exchange(behind(piece, crossed[-1] if crossed else None), "snap", cut))
    own = pieces_of(upper, OWN_WIDTHS)
    lefts = turned(own, crossed)
    mate = []
    for width in MATE_WIDTHS:
        first = sum(piece.shape[1] for piece in mate)
        for piece in crossed:
            if first < piece.shape[1]:
                break
            first -= piece.shape[1]
        mate.append(lax.slice_in_dim(piece, first, first + width * quarter, axis=1))

    low = jnp.bitwise_and(masks, cut - 1)
    crossing = (masks >= cut).astype(jnp.int32)
    rounds = jnp.concatenate([low, crossing])
    me = lax.axis_index("space").astype(jnp.int32)[None]

    held = [{0: piece} for piece in own + mate]
    sent = {}
    halves, columns, back, keeps = [], [], [], []

    def add_batch():
        batch = [
            [[held[n][low] for low in range(cut)] for n in numbers]
            for numbers in BATCHES[len(halves)]
        ]
        if keeps:
            keeps.pop()(held[len(own) - 1][cut - 1])
        earlier = columns if halves else sent[cut // 2][:3][-1]
        choices = jnp.concatenate([behind(rounds, earlier), me])
        even, odd = products(choices, lefts, batch, scale_factor, 1)
        halves.append(halved(even, odd, 1))
        give = summed(halves[-1], None)
        back.append(exchange(give.astype(jnp.bfloat16), "snap", cut))

        def keep(first, then):
            even, odd = products(behind(choices, first), lefts, batch, scale_factor, 0)
            columns.append(summed(halved(even, odd, 1), (give, then)))

        keeps.append(partial(keep, odd))

    for piece, low, bit in hops_in_order(OWN_WIDTHS + MATE_WIDTHS, cut):
        earlier = sent.setdefault(bit, [])
        depth = 2 if bit == 1 and len(earlier) < 99 else 1
        ties = earlier[-depth] if len(earlier) >= depth else None
        held[piece][low | bit] = exchange(behind(held[piece][low], ties), "snap", bit)
        earlier.append(held[piece][low | bit])
        while len(halves) < len(BATCHES) and all(
            len(held[n]) == cut for numbers in BATCHES[len(halves)] for n in numbers
        ):
            add_batch()
    keeps.pop()(None)
    results = [kept + got.astype(jnp.float32) for kept, got in zip(columns, back)]
    return jnp.concatenate(results, axis=2)[:, None]


def solution(mesh):
    in_specs = (P("space", "snap"), P("space"), P())
    out_specs = P(None, "snap", "space", None)
    return jax.shard_map(body, mesh=mesh, in_specs=in_specs, out_specs=out_specs, check_vma=False)
```
